256 devices in a mesh: dp: 2 (over core), seq: 16 (over z, y_hi), chan: 8 (over y_lo, x).
Axes of the slice: x: 4, y: 4 (y_hi: 2, y_lo: 2; y = y_hi * 2 + y_lo), z: 8, core: 2. Of those that a mesh axis runs over, the one named last changes fastest.
Arguments:
- features: bfloat16 [4096, 3, 8192], P(('dp', 'seq'), None, 'chan'), parts along dimension 0, may hold values from -6 to 6
- lengths: int32 [6], P('dp'), parts along dimension 0, may hold values from 1 to 1024, 2048 in all
- ids: int32 [4096], P(('dp', 'seq')), parts along dimension 0, may hold values from 0 to 511
- taps: float32 [3, 3, 8192], P(None, None, 'chan'), may hold values from -3.5 to 3.5
- filters: float32 [8192, 2048], P(('chan', 'seq')), as said below
- skip: float32 [8192], P(('chan', 'seq')), may hold values from 0.5 to 1.5
- out_weight: bfloat16 [8192, 8192], P('chan', 'seq'), may hold values from -0.0625 to 0.0625
- embedding: bfloat16 [512, 8192], P(None, 'chan'), may hold values from -6 to 6
Outputs:
- mixed: bfloat16 [4096, 8192], P(('dp', 'seq'), 'chan'), parts along dimension 0
The draws below stay inside these ranges and needn't reach their ends.
There are 2 independent parts, one for each index of `dp`. The reference program is written for one: setup_inputs(seed, part) draws one part's arguments, and reference() takes and returns one part's arrays. A program takes and returns all parts, laid end to end along the dimension named above; an argument that names none is the same for every part. Nothing has to cross between parts.
Inputs may be any that keep to these rules, and one draw needn't show every extreme that they name: `lengths`: the 3 documents fill the segment one after another and sum to 2048; the longest holds exactly 1024 positions. `filters`: positive.
All inputs are finite; a program needn't handle non-finite values.
Results may differ from the reference program's by a relative error of at most 0.022.
Values may be sent and summed in bfloat16 or wider, within the bound.
A program may use at most 128 MiB of HBM per device.

```python
import math
import jax
import jax.numpy as jnp
import numpy as np
from jax import lax

HIDDEN_DIM = 8192
VOCAB = 512
TOK_DEV = 128
SHORT = 3
DOCS = 3
SPAN_SIZE = 2048


def draw_filters(key, part):
    key = jax.random.fold_in(key, 17)
    subkeys = jax.random.split(key, 6)
    fast_share = 0.5
    rough_low = 0.5
    nucleotide_offsets = jnp.arange(SPAN_SIZE, dtype=jnp.float32)
    chosen = jax.random.uniform(subkeys[0], (HIDDEN_DIM,), dtype=jnp.float32) < fast_share
    slow_rate = jnp.exp(jax.random.uniform(subkeys[1], (HIDDEN_DIM,), dtype=jnp.float32, minval=math.log(0.1), maxval=0.0)) * (math.log(10.0) / SPAN_SIZE)
    fast_span = min(40, TOK_DEV // 2)
    fast_rate = jax.random.uniform(subkeys[2], (HIDDEN_DIM,), dtype=jnp.float32, minval=0.8, maxval=1.25) / fast_span
    falloff_speed = jnp.where(chosen, fast_rate, slow_rate)
    kernel_magnitude = jnp.sqrt(2.0 * falloff_speed / (1.0 - jnp.exp(-2.0 * falloff_speed * SPAN_SIZE)))
    flagged_loci = jax.random.uniform(subkeys[3], (HIDDEN_DIM, 3), dtype=jnp.float32, minval=0.0, maxval=float(SPAN_SIZE))
    omission_occurrences = jax.random.uniform(subkeys[4], (HIDDEN_DIM, 3), dtype=jnp.float32, minval=0.5, maxval=0.8)
    spike_occurrences = jnp.ones((HIDDEN_DIM, SPAN_SIZE), jnp.float32)
    for picked_entry in range(3):
        spike_occurrences = spike_occurrences * jnp.where(nucleotide_offsets[None, :] >= flagged_loci[:, picked_entry:picked_entry + 1], omission_occurrences[:, picked_entry:picked_entry + 1], 1.0)
    waveform_jaggedness = jax.random.uniform(subkeys[5], (HIDDEN_DIM, SPAN_SIZE), dtype=jnp.float32, minval=rough_low, maxval=2.0 - rough_low)
    return kernel_magnitude[:, None] * jnp.exp(-falloff_speed[:, None] * nucleotide_offsets[None, :]) * spike_occurrences * waveform_jaggedness


def touch_ends(result, key, smallest, top_value):
    index_at = [jax.random.randint(jax.random.fold_in(key, axis), (), 0, length) for axis, length in enumerate(result.shape)]
    longest = result.shape.index(max(result.shape))
    beside = index_at[:longest] + [(index_at[longest] + 1) % result.shape[longest]] + index_at[longest + 1:]
    return result.at[tuple(index_at)].set(smallest).at[tuple(beside)].set(top_value)


def level_of(rng, dims, shards, smallest, top_value):
    def one(position, blocks):
        steps = jax.random.uniform(jax.random.fold_in(jax.random.fold_in(rng, 6), position), (blocks,), jnp.float32, smallest / len(shards), top_value / len(shards))
        return jnp.repeat(jnp.exp(steps), dims[position] // blocks).reshape((-1,) + (1,) * (len(dims) - position - 1))

    gain = one(*shards[0])
    for cut in shards[1:]:
        gain = gain * one(*cut)
    return gain


def rank_table(number_of, slope):
    weights = [(1 << 20) // math.isqrt(rank ** slope) + 1 for rank in range(1, number_of + 1)]
    deviation = 1 + sum(weights) // (1 << 30)
    return np.cumsum(np.array([max(1, weight // deviation) for weight in weights]))


def skewed_ids(rng, dims, number_of, skew):
    grid = rank_table(number_of, skew)
    ticket = jax.random.randint(jax.random.fold_in(rng, 1), dims, 0, int(grid[number_of - 1]))
    grade = jnp.searchsorted(jnp.asarray(grid, jnp.int32), ticket, side="right")
    return jax.random.permutation(jax.random.fold_in(rng, 2), number_of)[grade].astype(jnp.int32)


def profile(count, total, limit, slope):
    weights = [(1 << 20) // math.isqrt(standing ** slope) + 1 for standing in range(2, count + 1)]
    rest, given = total - limit - (count - 1), [1] * (count - 1)
    while rest > 0:
        free = [i for i in range(count - 1) if given[i] < limit]
        mass, remaining = sum([weights[i] for i in free]), rest
        for i in free:
            extra = min(limit - given[i], max(1, remaining * weights[i] // mass), rest)
            given[i] = given[i] + extra
            rest = rest - extra
    return np.array([limit] + given)


def ragged(key, count, total, limit, lean):
    if count == 2:
        one = jax.random.randint(key, (), max(1, total - limit), min(limit, total - 1) + 1)
        return jnp.stack([one, total - one])
    sizes = jnp.asarray(profile(count, total, limit, lean), jnp.int32)
    couples = (count - 1) // 2
    giver, sink = sizes[1:1 + 2 * couples:2], sizes[2:2 + 2 * couples:2]
    room = jnp.minimum(giver - 1, limit - sink)
    passed = jax.random.randint(jax.random.fold_in(key, 1), (couples,), 0, 1 << 20) % (room + 1)
    sizes = sizes.at[1:1 + 2 * couples:2].set(giver - passed).at[2:2 + 2 * couples:2].set(sink + passed)
    return sizes[jax.random.permutation(jax.random.fold_in(key, 2), count)]


def bell_draw(rng, shape, scale, reach, cuts=(), kind=jnp.bfloat16):
    array = jax.random.normal(rng, shape, jnp.float32) * scale
    if len(cuts) > 0:
        array = level_of(rng, shape, cuts, -0.22, 0.18) * array
    return jnp.clip(array, min=-reach, max=reach).astype(kind)


def setup_inputs(seed: int = 0, part: int = 0) -> dict:
    streams_of = jax.random.split(jax.random.key(seed), 9)
    own_keys = jax.random.split(jax.random.fold_in(streams_of[8], part), 9)
    features = bell_draw(own_keys[0], (SPAN_SIZE, 3, HIDDEN_DIM), 1.0, 6.0, ((0, 16), (2, 8)))
    lengths = ragged(own_keys[1], DOCS, SPAN_SIZE, SPAN_SIZE // 2, 1).astype(jnp.int32)
    ids = touch_ends(skewed_ids(own_keys[2], (SPAN_SIZE,), VOCAB, 2), jax.random.fold_in(own_keys[2], 3), 0, VOCAB - 1).astype(jnp.int32)
    taps = bell_draw(streams_of[3], (SHORT, 3, HIDDEN_DIM), SHORT ** -0.5, 3.5, ((2, 8),), jnp.float32)
    filters = draw_filters(jax.random.fold_in(streams_of[8], 71), part)
    skip = jnp.clip(0.5 + 1.0 * jax.random.uniform(streams_of[5], (HIDDEN_DIM,), jnp.float32) ** level_of(streams_of[5], (HIDDEN_DIM,), ((0, 128),), -0.2, 0.2), 0.5, 1.5)
    out_weight = bell_draw(streams_of[6], (HIDDEN_DIM, HIDDEN_DIM), HIDDEN_DIM ** -0.5, 0.0625, ((0, 8), (1, 16)))
    embedding = bell_draw(streams_of[7], (VOCAB, HIDDEN_DIM), 1.0, 6.0, ((1, 8),))
    return dict(features=features, lengths=lengths, ids=ids, taps=taps, filters=filters, skip=skip, out_weight=out_weight, embedding=embedding)


def document_index(lengths, extent):
    bounds = jnp.cumsum(lengths).astype(jnp.int32)
    places = jnp.arange(extent, dtype=jnp.int32)
    return jnp.sum((places[:, None] >= bounds[None, :]).astype(jnp.int32), axis=1)


def reference(features, lengths, ids, taps, filters, skip, out_weight, embedding):
    documents = document_index(lengths, SPAN_SIZE)
    block_width = min(512, HIDDEN_DIM)
    block_count = HIDDEN_DIM // block_width
    feature_blocks = features.reshape(SPAN_SIZE, 3, block_count, block_width).transpose(2, 0, 1, 3)
    tap_blocks = taps.reshape(SHORT, 3, block_count, block_width).transpose(2, 0, 1, 3)
    filter_blocks = filters.reshape(block_count, block_width, SPAN_SIZE)
    skip_blocks = skip.reshape(block_count, block_width)
    doc_masks = (documents[None, :] == jnp.arange(DOCS, dtype=jnp.int32)[:, None]).astype(jnp.float32)

    def one_block(inputs):
        feature_block, tap_block, filter_block, skip_block = inputs
        values = feature_block.astype(jnp.float32)
        running = tap_block[0] * values
        for offset in range(1, SHORT):
            shifted = jnp.concatenate([jnp.zeros((offset, 3, block_width), jnp.float32), values[:SPAN_SIZE - offset]], axis=0)
            agreement = jnp.concatenate([jnp.zeros((offset,), jnp.float32), (documents[offset:] == documents[:SPAN_SIZE - offset]).astype(jnp.float32)])
            running = running + tap_block[offset] * shifted * agreement[:, None, None]
        shortconv = running.astype(jnp.bfloat16)
        product = (shortconv[:, 1].astype(jnp.float32) * shortconv[:, 2].astype(jnp.float32)).astype(jnp.bfloat16)
        signal = product.astype(jnp.float32).T
        masked = doc_masks[:, None, :] * signal[None]
        spectrum = jnp.fft.rfft(masked, n=2 * SPAN_SIZE, axis=-1)
        response = jnp.fft.rfft(filter_block, n=2 * SPAN_SIZE, axis=-1)
        restored = jnp.fft.irfft(spectrum * response[None], n=2 * SPAN_SIZE, axis=-1)[..., :SPAN_SIZE]
        longconv = jnp.sum(restored * doc_masks[:, None, :], axis=0)
        convolved = (longconv + skip_block[:, None] * signal).astype(jnp.bfloat16)
        gated_rows = (shortconv[:, 0].astype(jnp.float32) * convolved.T.astype(jnp.float32)).astype(jnp.bfloat16)
        return gated_rows

    gated_rows = lax.map(one_block, (feature_blocks, tap_blocks, filter_blocks, skip_blocks))
    gated_rows = gated_rows.transpose(1, 0, 2).reshape(SPAN_SIZE, HIDDEN_DIM)
    projected = jnp.dot(gated_rows, out_weight, preferred_element_type=jnp.float32)
    return (projected + embedding[ids].astype(jnp.float32)).astype(jnp.bfloat16)
```

```python
import jax
import jax.numpy as jnp
from jax import lax
from jax.experimental import pallas as pl
from jax.experimental.pallas import tpu as pltpu
from jax.sharding import PartitionSpec as P

MESH = pl.DeviceIdType.MESH
F32, BF16 = jnp.float32, jnp.bfloat16
B = 128
SEQ, CHAN, Z = 16, 8, 8
OWN = 64
LAGS = 8
PITCH = 65


def build_toeplitz(filt_ref, toep_ref, first, last):
    row = lax.broadcasted_iota(jnp.int32, (B, B), 0)
    col = lax.broadcasted_iota(jnp.int32, (B, B), 1)
    upper = col >= row

    def step(g, _):
        taps = filt_ref[pl.ds(pl.multiple_of(g * 8, 8), 8), :]
        for j in range(8):
            before = jnp.zeros((B, B), F32)
            for d in range(LAGS + 1):
                if d < LAGS:
                    line = jnp.broadcast_to(taps[j : j + 1, d * B : (d + 1) * B], (B, B))
                    now = pltpu.roll(line, 0, 1, stride=1, stride_axis=0)
                else:
                    now = jnp.zeros((B, B), F32)
                toep_ref[g * 8 + j, d * B : (d + 1) * B, :] = jnp.where(upper, now, before).astype(BF16)
                before = now
        return 0

    lax.fori_loop(first, last, step, 0)


def document(position, b1, b2):
    return (position >= b1).astype(jnp.int32) + (position >= b2).astype(jnp.int32)


def short_convolve(feat_ref, taps_ref, halo_ref, cols_ref, s, b1, b2):
    row = lax.broadcasted_iota(jnp.int32, (B, B), 0)
    position = s * B + row
    here = document(position, b1, b2)
    agree1 = ((document(position - 1, b1, b2) == here) & (position >= 1)).astype(F32)
    agree2 = ((document(position - 2, b1, b2) == here) & (position >= 2)).astype(F32)
    for n in range(8):
        cols = slice(n * B, (n + 1) * B)
        halo = halo_ref[:, cols].astype(F32)
        short = []
        for g in range(3):
            x = feat_ref[g, :, cols].astype(F32)
            older, newer = halo[2 * g : 2 * g + 1], halo[2 * g + 1 : 2 * g + 2]
            x1 = jnp.where(row < 1, newer, pltpu.roll(x, 1, 0))
            x2 = jnp.where(row < 1, older, jnp.where(row < 2, newer, pltpu.roll(x, 2, 0)))
            t = taps_ref[:, g, cols]
            running = t[0:1] * x + t[1:2] * x1 * agree1 + t[2:3] * x2 * agree2
            short.append(running.astype(BF16))
        product = (short[1].astype(F32) * short[2].astype(F32)).astype(BF16).T
        query = short[0].T
        for h in range(2):
            cols_ref[2 * n + h, 0:OWN, :] = product[h * OWN : (h + 1) * OWN]
            cols_ref[2 * n + h, OWN:B, :] = query[h * OWN : (h + 1) * OWN]


def long_convolve(toep_ref, x_ref, y_ref, b1, b2):
    block = lax.broadcasted_iota(jnp.int32, (SEQ, B), 0)
    lane = lax.broadcasted_iota(jnp.int32, (SEQ, B), 1)

    def docs(d):
        return document((block - d) * B + lane, b1, b2)

    masks = [[(docs(d) == k).astype(F32).astype(BF16) for d in range(LAGS + 1)] for k in range(3)]
    here = docs(0)

    def step(c, _):
        lhs = []
        for d in range(LAGS + 1):
            x = x_ref[pl.ds((LAGS - d) * PITCH + c, SEQ, stride=PITCH), :].astype(BF16)
            lhs.append(jnp.concatenate([masks[k][d] * x for k in range(3)], axis=0))
        y = jnp.dot(jnp.concatenate(lhs, axis=1), toep_ref[c], preferred_element_type=F32)
        y_ref[pl.ds(c, SEQ, stride=PITCH), :] = jnp.where(
            here == 0, y[0:SEQ], jnp.where(here == 1, y[SEQ : 2 * SEQ], y[2 * SEQ : 3 * SEQ])
        )
        return 0

    lax.fori_loop(0, OWN, step, 0, unroll=8)


def kernel(
    len_ref, feat_ref, taps_ref, filt_ref, skip_ref, w_ref, ids_ref, emb_ref, out_ref,
    halo_out, halo_in, cols_ref, rows_ref, toep_ref, x_ref, y_ref, gated_ref, wt_ref, g_ref,
    part_ref, got_ref, sum_ref, plane_ref, last_ref, look_ref,
    halo_s, halo_r, w_s, w_r, a_s, a_r, y_s, y_r, up_s, up_r, down_s, down_r, rs_s, rs_r, z_s, z_r, f_s, f_r,
):
    dp = lax.axis_index("dp")
    s = lax.axis_index("seq")
    k = lax.axis_index("chan")
    z, half = s // 2, s % 2
    b1 = len_ref[0]
    b2 = b1 + len_ref[1]

    def remote(src, dst, send, recv, seq, chan):
        return pltpu.make_async_remote_copy(
            src_ref=src, dst_ref=dst, send_sem=send, recv_sem=recv, device_id=(dp, seq, chan), device_id_type=MESH
        )

    barrier = pltpu.get_barrier_semaphore()
    for d in range(1, SEQ):
        pl.semaphore_signal(barrier, inc=1, device_id=(dp, (s + d) % SEQ, k), device_id_type=MESH)
    for d in range(1, CHAN):
        pl.semaphore_signal(barrier, inc=1, device_id=(dp, s, (k + d) % CHAN), device_id_type=MESH)

    for a in range(8):
        for b in range(4):
            wt_ref[half * 4 + b, :, a * B : (a + 1) * B] = w_ref[a * B : (a + 1) * B, b * B : (b + 1) * B].T
    edge = [feat_ref[g, B - 16 : B, :].astype(F32)[14:16] for g in range(3)]
    halo_out[...] = jnp.concatenate(edge + [jnp.zeros((10, CHAN * B), F32)], axis=0).astype(BF16)
    pl.semaphore_wait(barrier, SEQ - 1 + CHAN - 1)

    halo_copy = remote(halo_out, halo_in, halo_s, halo_r, (s + 1) % SEQ, k)
    halo_copy.start()
    mine = wt_ref.at[pl.ds(half * 4, 4)]
    w_copy = remote(mine, mine, w_s, w_r, z * 2 + 1 - half, k)
    w_copy.start()
    build_toeplitz(filt_ref, toep_ref, 0, 2)
    halo_copy.wait()
    short_convolve(feat_ref, taps_ref, halo_in, cols_ref, s, b1, b2)

    spread = []
    for d in range(1, SEQ):
        to = (s + d) % SEQ
        copy = remote(cols_ref.at[to], rows_ref.at[s], a_s.at[d], a_r.at[d], to, k)
        copy.start()
        spread.append(copy)
    rows_ref[s] = cols_ref[s]
    build_toeplitz(filt_ref, toep_ref, 2, 8)

    wanted = jnp.broadcast_to(ids_ref[...], (B, B)).T
    lane = lax.broadcasted_iota(jnp.int32, (B, B), 1)
    vocab = emb_ref.shape[0] // B
    hot = jnp.concatenate([(wanted == lane + v * B).astype(F32).astype(BF16) for v in range(vocab)], axis=1)
    for n in range(8):
        cols = slice(n * B, (n + 1) * B)
        look_ref[:, cols] = jnp.dot(hot, emb_ref[:, cols], preferred_element_type=F32).astype(BF16)
    skip = jnp.broadcast_to(skip_ref[...], (B, OWN)).T

    for copy in spread:
        copy.wait()
    x_ref[0 : LAGS * PITCH, :] = jnp.zeros((LAGS * PITCH, B), F32)
    for i in range(SEQ):
        at = (LAGS + i) * PITCH
        x_ref[at : at + OWN, :] = rows_ref[i, 0:OWN, :].astype(F32)
    long_convolve(toep_ref, x_ref, y_ref, b1, b2)
    for i in range(SEQ):
        signal = rows_ref[i, 0:OWN, :].astype(F32)
        convolved = (y_ref[i * PITCH : i * PITCH + OWN, :] + skip * signal).astype(BF16)
        gated = rows_ref[i, OWN:B, :].astype(F32) * convolved.astype(F32)
        place = i // 2 // 2 + 4 * (i // 2 % 2)
        gated_ref[i % 2, place] = gated.astype(BF16)

    mate = []
    for j in range(4):
        copy = remote(
            gated_ref.at[1 - half, pl.ds(2 * j, 2)], g_ref.at[pl.ds(2 * j, 2), z, half], y_s.at[j], y_r.at[j],
            z * 2 + 1 - half, k,
        )
        copy.start()
        mate.append(copy)
    for q in range(8):
        g_ref[q, z, half] = gated_ref[half, q]

    up_seq, down_seq = (z + 1) % Z * 2 + half, (z + Z - 1) % Z * 2 + half

    def up(j, n):
        block = g_ref.at[pl.ds(2 * j, 2), (z + Z - n + 1) % Z]
        return remote(block, block, up_s.at[j, n], up_r.at[j, n], up_seq, k)

    def down(j, n):
        block = g_ref.at[pl.ds(2 * j, 2), (z + n - 1) % Z]
        return remote(block, block, down_s.at[j, n], down_r.at[j, n], down_seq, k)

    def up_has(j, n):
        return n <= 3 + (j % 2 == 0)

    def down_has(j, n):
        return n <= 3 + (j % 2 == 1)

    def own(j):
        mate[j].wait_recv()
        up(j, 1).start()
        down(j, 1).start()

    def forward(j, n):
        if up_has(j, n):
            up(j, n).wait_recv()
            if up_has(j, n + 1):
                up(j, n + 1).start()
        if down_has(j, n):
            down(j, n).wait_recv()
            if down_has(j, n + 1):
                down(j, n + 1).start()

    sent = []

    def project(t):
        rhs = jnp.concatenate([g_ref[4 * t + q].reshape(Z * B, B) for q in range(4)], axis=1)
        for d in [1, 7, 2, 6, 3, 5, 4, 0]:
            to = (k + d) % CHAN
            value = jnp.dot(wt_ref[to], rhs, preferred_element_type=F32).astype(BF16)
            for q in range(4):
                part_ref[t, d, q] = value[:, q * B : (q + 1) * B]
            if d:
                copy = remote(part_ref.at[t, d], got_ref.at[t, d], rs_s.at[t, d], rs_r.at[t, d], s, to)
                copy.start()
                sent.append((t, copy))

    def collect(t):
        for u, copy in sent:
            if u == t:
                copy.wait_recv()
        for q in range(4):
            total = part_ref[t, 0, q].astype(F32)
            for d in range(1, CHAN):
                total = total + got_ref[t, d, q].astype(F32)
            sum_ref[t, q] = total.T.astype(BF16)
        for q in range(4):
            to = 2 * q + t

            @pl.when(z != to)
            def _():
                remote(sum_ref.at[t, q], plane_ref.at[z], z_s.at[t, q], z_r.at[z], to * 2 + half, k).start()

            @pl.when(z == to)
            def _():
                plane_ref[to] = sum_ref[t, q]

    own(0)
    own(1)
    for n in (1, 2, 3):
        forward(0, n)
        forward(1, n)
    own(2)
    own(3)
    forward(0, 4)
    forward(1, 4)
    w_copy.wait()
    project(0)
    for n in (1, 2, 3, 4):
        forward(2, n)
        forward(3, n)
    project(1)
    collect(0)
    collect(1)

    for zz in range(Z):

        @pl.when(z != zz)
        def _():
            remote(sum_ref.at[0, 0], plane_ref.at[zz], z_s.at[0, 0], z_r.at[zz], zz * 2 + half, k).wait_recv()

        @pl.when(k != zz)
        def _():
            remote(plane_ref.at[zz], last_ref.at[k], f_s.at[zz], f_r.at[k], s, zz).start()

        @pl.when(k == zz)
        def _():
            last_ref[zz] = plane_ref[zz]

    for kk in range(CHAN):

        @pl.when(k != kk)
        def _():
            remote(plane_ref.at[0], last_ref.at[kk], f_s.at[0], f_r.at[kk], s, kk).wait_recv()

        cols = slice(kk * B, (kk + 1) * B)
        out_ref[:, cols] = (last_ref[kk].astype(F32) + look_ref[:, cols].astype(F32)).astype(BF16)

    for copy in mate:
        copy.wait_send()
    for j in range(4):
        for n in range(1, 5):
            if up_has(j, n):
                up(j, n).wait_send()
            if down_has(j, n):
                down(j, n).wait_send()
    for _, copy in sent:
        copy.wait_send()
    for t in range(2):
        for q in range(4):

            @pl.when(z != 2 * q + t)
            def _():
                remote(sum_ref.at[t, q], plane_ref.at[z], z_s.at[t, q], z_r.at[z], 2 * (2 * q + t) + half, k).wait_send()

    for zz in range(Z):

        @pl.when(k != zz)
        def _():
            remote(plane_ref.at[zz], last_ref.at[k], f_s.at[zz], f_r.at[k], s, zz).wait_send()


def local(features, lengths, ids, taps, filters, skip, out_weight, embedding):
    vmem = pl.BlockSpec(memory_space=pltpu.VMEM)
    dma = pltpu.SemaphoreType.DMA
    tile = (B, B)
    return pl.pallas_call(
        kernel,
        out_shape=jax.ShapeDtypeStruct((B, CHAN * B), BF16),
        in_specs=[pl.BlockSpec(memory_space=pltpu.SMEM)] + [vmem] * 7,
        out_specs=vmem,
        scratch_shapes=[
            pltpu.VMEM((16, CHAN * B), BF16),
            pltpu.VMEM((16, CHAN * B), BF16),
            pltpu.VMEM((SEQ,) + tile, BF16),
            pltpu.VMEM((SEQ,) + tile, BF16),
            pltpu.VMEM((OWN, (LAGS + 1) * B, B), BF16),
            pltpu.VMEM(((LAGS + SEQ) * PITCH, B), F32),
            pltpu.VMEM((SEQ * PITCH, B), F32),
            pltpu.VMEM((2, 8, OWN, B), BF16),
            pltpu.VMEM((8, B, CHAN * B), BF16),
            pltpu.VMEM((8, Z, 2, OWN, B), BF16),
            pltpu.VMEM((2, CHAN, 4) + tile, BF16),
            pltpu.VMEM((2, CHAN, 4) + tile, BF16),
            pltpu.VMEM((2, 4) + tile, BF16),
            pltpu.VMEM((Z,) + tile, BF16),
            pltpu.VMEM((CHAN,) + tile, BF16),
            pltpu.VMEM((B, CHAN * B), BF16),
            dma, dma, dma, dma,
            dma((SEQ,)), dma((SEQ,)),
            dma((4,)), dma((4,)),
            dma((4, 5)), dma((4, 5)), dma((4, 5)), dma((4, 5)),
            dma((2, CHAN)), dma((2, CHAN)),
            dma((2, 4)), dma((Z,)),
            dma((Z,)), dma((CHAN,)),
        ],
        compiler_params=pltpu.CompilerParams(
            collective_id=0, has_side_effects=True, vmem_limit_bytes=56 * 2**20
        ),
        name="hyena_block",
    )(
        lengths,
        features.transpose(1, 0, 2),
        taps,
        filters,
        skip.reshape(1, -1),
        out_weight,
        ids.reshape(1, -1),
        embedding,
    )


def solution(mesh):
    placed = (
        P(("dp", "seq"), None, "chan"),
        P("dp"),
        P(("dp", "seq")),
        P(None, None, "chan"),
        P(("chan", "seq"), None),
        P(("chan", "seq")),
        P("chan", "seq"),
        P(None, "chan"),
    )
    return jax.shard_map(
        local, mesh=mesh, in_specs=placed, out_specs=P(("dp", "seq"), "chan"), check_vma=False
    )
```

```python
import jax
import jax.numpy as jnp
from jax import lax
from jax.experimental import pallas as pl
from jax.experimental.pallas import tpu as pltpu
from jax.sharding import PartitionSpec as P

MESH = pl.DeviceIdType.MESH
F32, BF16 = jnp.float32, jnp.bfloat16
B = 128
SEQ, CHAN, Z = 16, 8, 8
OWN = 64
LAGS = 8
PITCH = 65


def build_toeplitz(filt_ref, toep_ref, first, last):
    row = lax.broadcasted_iota(jnp.int32, (B, B), 0)
    col = lax.broadcasted_iota(jnp.int32, (B, B), 1)
    upper = col >= row

    def step(g, _):
        taps = filt_ref[pl.ds(pl.multiple_of(g * 8, 8), 8), :]
        for j in range(8):
            before = jnp.zeros((B, B), F32)
            for d in range(LAGS + 1):
                if d < LAGS:
                    line = jnp.broadcast_to(taps[j : j + 1, d * B : (d + 1) * B], (B, B))
                    now = pltpu.roll(line, 0, 1, stride=1, stride_axis=0)
                else:
                    now = jnp.zeros((B, B), F32)
                toep_ref[g * 8 + j, d * B : (d + 1) * B, :] = jnp.where(upper, now, before).astype(BF16)
                before = now
        return 0

    lax.fori_loop(first, last, step, 0)


def document(position, b1, b2):
    return (position >= b1).astype(jnp.int32) + (position >= b2).astype(jnp.int32)


def short_convolve(feat_ref, taps_ref, halo_ref, cols_ref, s, b1, b2):
    row = lax.broadcasted_iota(jnp.int32, (B, B), 0)
    position = s * B + row
    here = document(position, b1, b2)
    agree1 = ((document(position - 1, b1, b2) == here) & (position >= 1)).astype(F32)
    agree2 = ((document(position - 2, b1, b2) == here) & (position >= 2)).astype(F32)
    for n in range(8):
        cols = slice(n * B, (n + 1) * B)
        halo = halo_ref[:, cols].astype(F32)
        short = []
        for g in range(3):
            x = feat_ref[g, :, cols].astype(F32)
            older, newer = halo[2 * g : 2 * g + 1], halo[2 * g + 1 : 2 * g + 2]
            x1 = jnp.where(row < 1, newer, pltpu.roll(x, 1, 0))
            x2 = jnp.where(row < 1, older, jnp.where(row < 2, newer, pltpu.roll(x, 2, 0)))
            t = taps_ref[:, g, cols]
            running = t[0:1] * x + t[1:2] * x1 * agree1 + t[2:3] * x2 * agree2
            short.append(running.astype(BF16))
        product = (short[1].astype(F32) * short[2].astype(F32)).astype(BF16).T
        query = short[0].T
        for h in range(2):
            cols_ref[2 * n + h, 0:OWN, :] = product[h * OWN : (h + 1) * OWN]
            cols_ref[2 * n + h, OWN:B, :] = query[h * OWN : (h + 1) * OWN]


def long_convolve(toep_ref, x_ref, y_ref, b1, b2):
    block = lax.broadcasted_iota(jnp.int32, (SEQ, B), 0)
    lane = lax.broadcasted_iota(jnp.int32, (SEQ, B), 1)

    def docs(d):
        return document((block - d) * B + lane, b1, b2)

    masks = [[(docs(d) == k).astype(F32).astype(BF16) for d in range(LAGS + 1)] for k in range(3)]
    here = docs(0)

    def step(c, _):
        lhs = []
        for d in range(LAGS + 1):
            x = x_ref[pl.ds((LAGS - d) * PITCH + c, SEQ, stride=PITCH), :].astype(BF16)
            lhs.append(jnp.concatenate([masks[k][d] * x for k in range(3)], axis=0))
        y = jnp.dot(jnp.concatenate(lhs, axis=1), toep_ref[c], preferred_element_type=F32)
        y_ref[pl.ds(c, SEQ, stride=PITCH), :] = jnp.where(
            here == 0, y[0:SEQ], jnp.where(here == 1, y[SEQ : 2 * SEQ], y[2 * SEQ : 3 * SEQ])
        )
        return 0

    lax.fori_loop(0, OWN, step, 0, unroll=8)


def kernel(
    len_ref, feat_ref, taps_ref, filt_ref, skip_ref, w_hbm, ids_ref, emb_hbm, out_ref,
    halo_out, halo_in, cols_ref, rows_ref, toep_ref, x_ref, y_ref, gated_ref, pair_ref, w_ref, emb_ref, g_ref,
    part_ref, got_ref, sum_ref, plane_ref, last_ref, look_ref,
    own_s, emb_s, halo_s, halo_r, w_s, w_r, sib_s, sib_r, p_s, p_r, q_s, q_r, y_s, y_r,
    up_s, up_r, down_s, down_r, rs_s, rs_r, z_s, z_r, f_s, f_r,
):
    dp = lax.axis_index("dp")
    s = lax.axis_index("seq")
    k = lax.axis_index("chan")
    z, half = s // 2, s % 2
    mate_seq = z * 2 + 1 - half

    barrier = pltpu.get_barrier_semaphore()
    for d in range(1, SEQ):
        pl.semaphore_signal(barrier, inc=1, device_id=(dp, (s + d) % SEQ, k), device_id_type=MESH)
    for d in range(1, CHAN):
        pl.semaphore_signal(barrier, inc=1, device_id=(dp, s, (k + d) % CHAN), device_id_type=MESH)
    pl.semaphore_signal(barrier, inc=1, device_id=(1 - dp, s, k), device_id_type=MESH)

    own_w = [
        pltpu.make_async_copy(w_hbm.at[:, pl.ds(b * B, B)], w_ref.at[half * 4 + b], own_s.at[b]) for b in range(4)
    ]
    emb_copy = pltpu.make_async_copy(emb_hbm, emb_ref, emb_s)
    for copy in own_w:
        copy.start()
    emb_copy.start()

    b1 = len_ref[0]
    b2 = b1 + len_ref[1]

    def remote(src, dst, send, recv, seq, chan, core=dp):
        return pltpu.make_async_remote_copy(
            src_ref=src, dst_ref=dst, send_sem=send, recv_sem=recv, device_id=(core, seq, chan), device_id_type=MESH
        )

    edge = [feat_ref[g, B - 16 : B, :].astype(F32)[14:16] for g in range(3)]
    halo_out[...] = jnp.concatenate(edge + [jnp.zeros((10, CHAN * B), F32)], axis=0).astype(BF16)
    pl.semaphore_wait(barrier, SEQ - 1 + CHAN - 1 + 1)

    halo_copy = remote(halo_out, halo_in, halo_s, halo_r, (s + 1) % SEQ, k)
    halo_copy.start()
    build_toeplitz(filt_ref, toep_ref, 0, 2)
    halo_copy.wait()
    short_convolve(feat_ref, taps_ref, halo_in, cols_ref, s, b1, b2)

    spread = []
    for rows, send, recv in ((pl.ds(0, OWN), p_s, p_r), (pl.ds(OWN, OWN), q_s, q_r)):
        for d in range(1, SEQ):
            to = (s + d) % SEQ
            copy = remote(cols_ref.at[to, rows], rows_ref.at[s, rows], send.at[d], recv.at[d], to, k)
            copy.start()
            spread.append(copy)
    rows_ref[s] = cols_ref[s]
    build_toeplitz(filt_ref, toep_ref, 2, 8)

    emb_copy.wait()
    wanted = jnp.broadcast_to(ids_ref[...], (B, B)).T
    lane = lax.broadcasted_iota(jnp.int32, (B, B), 1)
    vocab = emb_ref.shape[0] // B
    hot = jnp.concatenate([(wanted == lane + v * B).astype(F32).astype(BF16) for v in range(vocab)], axis=1)
    for n in range(8):
        cols = slice(n * B, (n + 1) * B)
        look_ref[:, cols] = jnp.dot(hot, emb_ref[:, cols], preferred_element_type=F32).astype(BF16)
    skip = jnp.broadcast_to(skip_ref[...], (B, OWN)).T

    for copy in spread[: SEQ - 1]:
        copy.wait()
    x_ref[0 : LAGS * PITCH, :] = jnp.zeros((LAGS * PITCH, B), F32)
    for i in range(SEQ):
        at = (LAGS + i) * PITCH
        x_ref[at : at + OWN, :] = rows_ref[i, 0:OWN, :].astype(F32)
    long_convolve(toep_ref, x_ref, y_ref, b1, b2)
    for copy in spread[SEQ - 1 :]:
        copy.wait()
    for i in range(SEQ):
        signal = rows_ref[i, 0:OWN, :].astype(F32)
        convolved = (y_ref[i * PITCH : i * PITCH + OWN, :] + skip * signal).astype(BF16)
        gated = rows_ref[i, OWN:B, :].astype(F32) * convolved.astype(F32)
        owner = i // 2
        gated_ref[i % 2, 2 * (owner % 4) + owner // 4] = gated.astype(BF16)

    mate = []
    for j in range(4):
        two = pl.ds(2 * j, 2)
        copy = remote(gated_ref.at[1 - half, two], pair_ref.at[two, half], y_s.at[j], y_r.at[j], mate_seq, k)
        copy.start()
        mate.append(copy)
    for copy in own_w:
        copy.wait()
    depth = w_ref.shape[1] // 2
    mine = w_ref.at[pl.ds(half * 4, 4), pl.ds(dp * depth, depth)]
    w_copy = remote(mine, mine, w_s, w_r, mate_seq, k)
    w_copy.start()
    theirs = w_ref.at[pl.ds((1 - half) * 4, 4), pl.ds(dp * depth, depth)]
    w_share = remote(theirs, theirs, sib_s, sib_r, s, k, 1 - dp)
    for q in range(8):
        pair_ref[q, half] = gated_ref[half, q]

    up_seq, down_seq = (z + 1) % Z * 2 + half, (z + Z - 1) % Z * 2 + half

    def up(j, n):
        block = g_ref.at[pl.ds(2 * j, 2), (z + Z - n + 1) % Z]
        return remote(block, block, up_s.at[j, n], up_r.at[j, n], up_seq, k)

    def down(j, n):
        block = g_ref.at[pl.ds(2 * j, 2), (z + n - 1) % Z]
        return remote(block, block, down_s.at[j, n], down_r.at[j, n], down_seq, k)

    def up_has(j, n):
        return n <= 3 + (j % 2 == 0)

    def down_has(j, n):
        return n <= 3 + (j % 2 == 1)

    def own(j):
        mate[j].wait_recv()
        for q in (2 * j, 2 * j + 1):
            g_ref[q, z] = pair_ref[q].reshape(B, B).T
        up(j, 1).start()
        down(j, 1).start()

    def forward(j, n):
        if up_has(j, n):
            up(j, n).wait_recv()
            if up_has(j, n + 1):
                up(j, n + 1).start()
        if down_has(j, n):
            down(j, n).wait_recv()
            if down_has(j, n + 1):
                down(j, n + 1).start()

    sent = []

    def project(j):
        lhs = jnp.concatenate(
            [jnp.concatenate([g_ref[q, zz] for zz in range(Z)], axis=1) for q in (2 * j, 2 * j + 1)], axis=0
        )
        for pair in ((1, 7), (2, 6), (3, 5), (4, 0)):
            rhs = jnp.concatenate([w_ref[(k + d) % CHAN] for d in pair], axis=1)
            value = jnp.dot(lhs, rhs, preferred_element_type=F32).astype(BF16)
            for n, d in enumerate(pair):
                for q in range(2):
                    part_ref[j, d, q] = value[q * B : (q + 1) * B, n * B : (n + 1) * B]
                if d:
                    copy = remote(
                        part_ref.at[j, d], got_ref.at[j, d], rs_s.at[j, d], rs_r.at[j, d], s, (k + d) % CHAN
                    )
                    copy.start()
                    sent.append((j, copy))

    def to_plane(j, q):
        owner = j + 4 * q
        return owner, remote(sum_ref.at[j, q], plane_ref.at[z], z_s.at[j, q], z_r.at[z], owner * 2 + half, k)

    def collect(j):
        for u, copy in sent:
            if u == j:
                copy.wait_recv()
        for q in range(2):
            total = part_ref[j, 0, q].astype(F32)
            for d in range(1, CHAN):
                total = total + got_ref[j, d, q].astype(F32)
            sum_ref[j, q] = total.astype(BF16)
            owner, copy = to_plane(j, q)

            @pl.when(z != owner)
            def _():
                copy.start()

            @pl.when(z == owner)
            def _():
                plane_ref[owner] = sum_ref[j, q]

    own(0)
    own(1)
    forward(0, 1)
    own(2)
    forward(1, 1)
    forward(0, 2)
    own(3)
    forward(2, 1)
    forward(1, 2)
    forward(0, 3)
    forward(3, 1)
    w_copy.wait_recv()
    w_share.start()
    forward(2, 2)
    forward(1, 3)
    forward(0, 4)
    forward(3, 2)
    w_share.wait_recv()
    project(0)
    forward(2, 3)
    forward(1, 4)
    forward(3, 3)
    project(1)
    forward(2, 4)
    project(2)
    forward(3, 4)
    project(3)
    for j in range(4):
        collect(j)

    for zz in range(Z):

        @pl.when(z != zz)
        def _():
            remote(sum_ref.at[0, 0], plane_ref.at[zz], z_s.at[0, 0], z_r.at[zz], zz * 2 + half, k).wait_recv()

        @pl.when(k != zz)
        def _():
            remote(plane_ref.at[zz], last_ref.at[k], f_s.at[zz], f_r.at[k], s, zz).start()

        @pl.when(k == zz)
        def _():
            last_ref[zz] = plane_ref[zz]

    for kk in range(CHAN):

        @pl.when(k != kk)
        def _():
            remote(plane_ref.at[0], last_ref.at[kk], f_s.at[0], f_r.at[kk], s, kk).wait_recv()

        cols = slice(kk * B, (kk + 1) * B)
        out_ref[:, cols] = (last_ref[kk].astype(F32) + look_ref[:, cols].astype(F32)).astype(BF16)

    for copy in mate:
        copy.wait_send()
    w_copy.wait_send()
    w_share.wait_send()
    for j in range(4):
        for n in range(1, 5):
            if up_has(j, n):
                up(j, n).wait_send()
            if down_has(j, n):
                down(j, n).wait_send()
    for _, copy in sent:
        copy.wait_send()
    for j in range(4):
        for q in range(2):
            owner, copy = to_plane(j, q)

            @pl.when(z != owner)
            def _():
                copy.wait_send()

    for zz in range(Z):

        @pl.when(k != zz)
        def _():
            remote(plane_ref.at[zz], last_ref.at[k], f_s.at[zz], f_r.at[k], s, zz).wait_send()


def local(features, lengths, ids, taps, filters, skip, out_weight, embedding):
    vmem = pl.BlockSpec(memory_space=pltpu.VMEM)
    hbm = pl.BlockSpec(memory_space=pl.ANY)
    dma = pltpu.SemaphoreType.DMA
    tile = (B, B)
    return pl.pallas_call(
        kernel,
        out_shape=jax.ShapeDtypeStruct((B, CHAN * B), BF16),
        in_specs=[pl.BlockSpec(memory_space=pltpu.SMEM), vmem, vmem, vmem, vmem, hbm, vmem, hbm],
        out_specs=vmem,
        scratch_shapes=[
            pltpu.VMEM((16, CHAN * B), BF16),
            pltpu.VMEM((16, CHAN * B), BF16),
            pltpu.VMEM((SEQ,) + tile, BF16),
            pltpu.VMEM((SEQ,) + tile, BF16),
            pltpu.VMEM((OWN, (LAGS + 1) * B, B), BF16),
            pltpu.VMEM(((LAGS + SEQ) * PITCH, B), F32),
            pltpu.VMEM((SEQ * PITCH, B), F32),
            pltpu.VMEM((2, 8, OWN, B), BF16),
            pltpu.VMEM((8, 2, OWN, B), BF16),
            pltpu.VMEM((CHAN, CHAN * B, B), BF16),
            pltpu.VMEM(embedding.shape, BF16),
            pltpu.VMEM((8, Z) + tile, BF16),
            pltpu.VMEM((4, CHAN, 2) + tile, BF16),
            pltpu.VMEM((4, CHAN, 2) + tile, BF16),
            pltpu.VMEM((4, 2) + tile, BF16),
            pltpu.VMEM((Z,) + tile, BF16),
            pltpu.VMEM((CHAN,) + tile, BF16),
            pltpu.VMEM((B, CHAN * B), BF16),
            dma((4,)), dma,
            dma, dma, dma, dma, dma, dma,
            dma((SEQ,)), dma((SEQ,)), dma((SEQ,)), dma((SEQ,)),
            dma((4,)), dma((4,)),
            dma((4, 5)), dma((4, 5)), dma((4, 5)), dma((4, 5)),
            dma((4, CHAN)), dma((4, CHAN)),
            dma((4, 2)), dma((Z,)),
            dma((Z,)), dma((CHAN,)),
        ],
        compiler_params=pltpu.CompilerParams(
            collective_id=0, has_side_effects=True, vmem_limit_bytes=56 * 2**20
        ),
        name="hyena_block",
    )(
        lengths,
        features.transpose(1, 0, 2),
        taps,
        filters,
        skip.reshape(1, -1),
        out_weight,
        ids.reshape(1, -1),
        embedding,
    )


def solution(mesh):
    placed = (
        P(("dp", "seq"), None, "chan"),
        P("dp"),
        P(("dp", "seq")),
        P(None, None, "chan"),
        P(("chan", "seq"), None),
        P(("chan", "seq")),
        P("chan", "seq"),
        P(None, "chan"),
    )
    return jax.shard_map(
        local, mesh=mesh, in_specs=placed, out_specs=P(("dp", "seq"), "chan"), check_vma=False
    )
```

```python
import jax
import jax.numpy as jnp
from jax import lax
from jax.experimental import pallas as pl
from jax.experimental.pallas import tpu as pltpu
from jax.sharding import PartitionSpec as P

MESH = pl.DeviceIdType.MESH
F32, BF16 = jnp.float32, jnp.bfloat16
B = 128
SEQ, CHAN, Z = 16, 8, 8
OWN = 64
LAGS = 8
PITCH = 65


def build_toeplitz(filt_ref, toep_ref, first, last):
    row = lax.broadcasted_iota(jnp.int32, (B, B), 0)
    col = lax.broadcasted_iota(jnp.int32, (B, B), 1)
    upper = col >= row

    def step(g, _):
        taps = filt_ref[pl.ds(pl.multiple_of(g * 8, 8), 8), :]
        for j in range(8):
            before = jnp.zeros((B, B), F32)
            for d in range(LAGS + 1):
                if d < LAGS:
                    line = jnp.broadcast_to(taps[j : j + 1, d * B : (d + 1) * B], (B, B))
                    now = pltpu.roll(line, 0, 1, stride=1, stride_axis=0)
                else:
                    now = jnp.zeros((B, B), F32)
                toep_ref[g * 8 + j, d * B : (d + 1) * B, :] = jnp.where(upper, now, before).astype(BF16)
                before = now
        return 0

    lax.fori_loop(first, last, step, 0)


def document(position, b1, b2):
    return (position >= b1).astype(jnp.int32) + (position >= b2).astype(jnp.int32)


def short_agreement(s, b1, b2):
    row = lax.broadcasted_iota(jnp.int32, (B, B), 0)
    position = s * B + row
    here = document(position, b1, b2)
    agree1 = ((document(position - 1, b1, b2) == here) & (position >= 1)).astype(F32)
    agree2 = ((document(position - 2, b1, b2) == here) & (position >= 2)).astype(F32)
    return row, agree1, agree2


def short_convolve(feat_ref, taps_ref, halo_ref, agreement, g, n):
    row, agree1, agree2 = agreement
    cols = pl.ds(pl.multiple_of(n * B, B), B)
    x = feat_ref[g, :, cols].astype(F32)
    halo = halo_ref[:, cols].astype(F32)
    older, newer = halo[2 * g : 2 * g + 1], halo[2 * g + 1 : 2 * g + 2]
    x1 = jnp.where(row < 1, newer, pltpu.roll(x, 1, 0))
    x2 = jnp.where(row < 1, older, jnp.where(row < 2, newer, pltpu.roll(x, 2, 0)))
    t = [taps_ref[lag, pl.ds(g, 1), cols] for lag in range(3)]
    return (t[0] * x + t[1] * x1 * agree1 + t[2] * x2 * agree2).astype(BF16)


def long_convolve(toep_ref, x_ref, y_ref, b1, b2):
    block = lax.broadcasted_iota(jnp.int32, (SEQ, B), 0)
    lane = lax.broadcasted_iota(jnp.int32, (SEQ, B), 1)

    def docs(d):
        return document((block - d) * B + lane, b1, b2)

    masks = [[(docs(d) == k).astype(F32).astype(BF16) for d in range(LAGS + 1)] for k in range(3)]
    here = docs(0)

    def step(c, _):
        lhs = []
        for d in range(LAGS + 1):
            x = x_ref[pl.ds((LAGS - d) * PITCH + c, SEQ, stride=PITCH), :].astype(BF16)
            lhs.append(jnp.concatenate([masks[k][d] * x for k in range(3)], axis=0))
        y = jnp.dot(jnp.concatenate(lhs, axis=1), toep_ref[c], preferred_element_type=F32)
        y_ref[pl.ds(c, SEQ, stride=PITCH), :] = jnp.where(
            here == 0, y[0:SEQ], jnp.where(here == 1, y[SEQ : 2 * SEQ], y[2 * SEQ : 3 * SEQ])
        )
        return 0

    lax.fori_loop(0, OWN, step, 0, unroll=8)


def kernel(
    len_ref, feat_ref, taps_ref, filt_ref, skip_ref, w_hbm, ids_ref, emb_hbm, out_ref,
    halo_out, halo_in, cols_ref, rows_ref, toep_ref, x_ref, y_ref, gated_ref, pair_ref, w_ref, emb_ref, g_ref,
    part_y, part_x, got_y, got_x, mid_y, mid_x, end_y, end_x, sum_ref, plane_ref, last_ref, look_ref,
    own_s, emb_s, halo_s, halo_r, w_s, w_r, sib_s, sib_r, p_s, p_r, q_s, q_r, y_s, y_r,
    up_s, up_r, down_s, down_r, ya_s, ya_r, yb_s, yb_r, xa_s, xa_r, xb_s, xb_r, z_s, z_r, f_s, f_r,
):
    dp = lax.axis_index("dp")
    s = lax.axis_index("seq")
    k = lax.axis_index("chan")
    z, half = s // 2, s % 2
    mate_seq = z * 2 + 1 - half

    barrier = pltpu.get_barrier_semaphore()
    for d in range(1, SEQ):
        pl.semaphore_signal(barrier, inc=1, device_id=(dp, (s + d) % SEQ, k), device_id_type=MESH)
    for d in range(1, CHAN):
        pl.semaphore_signal(barrier, inc=1, device_id=(dp, s, (k + d) % CHAN), device_id_type=MESH)
    pl.semaphore_signal(barrier, inc=1, device_id=(1 - dp, s, k), device_id_type=MESH)

    own_w = [
        pltpu.make_async_copy(w_hbm.at[:, pl.ds(b * B, B)], w_ref.at[half * 4 + b], own_s.at[b]) for b in range(4)
    ]
    emb_copy = pltpu.make_async_copy(emb_hbm, emb_ref, emb_s)
    for copy in own_w:
        copy.start()
    emb_copy.start()

    b1 = len_ref[0]
    b2 = b1 + len_ref[1]

    def remote(src, dst, send, recv, seq, chan, core=dp):
        return pltpu.make_async_remote_copy(
            src_ref=src, dst_ref=dst, send_sem=send, recv_sem=recv, device_id=(core, seq, chan), device_id_type=MESH
        )

    edge = [feat_ref[g, B - 16 : B, :].astype(F32)[14:16] for g in range(3)]
    halo_out[...] = jnp.concatenate(edge + [jnp.zeros((10, CHAN * B), F32)], axis=0).astype(BF16)
    pl.semaphore_wait(barrier, SEQ - 1 + CHAN - 1 + 1)

    halo_copy = remote(halo_out, halo_in, halo_s, halo_r, (s + 1) % SEQ, k)
    halo_copy.start()
    for copy in own_w:
        copy.wait()
    depth = w_ref.shape[1] // 2
    mine = w_ref.at[pl.ds(half * 4, 4), pl.ds(dp * depth, depth)]
    w_copy = remote(mine, mine, w_s, w_r, mate_seq, k)
    theirs = w_ref.at[pl.ds((1 - half) * 4, 4), pl.ds(dp * depth, depth)]
    w_share = remote(theirs, theirs, sib_s, sib_r, s, k, 1 - dp)
    build_toeplitz(filt_ref, toep_ref, 0, 2)
    halo_copy.wait()
    agreement = short_agreement(s, b1, b2)

    def spread(n, e, rows, send, recv):
        to = (z + n) % Z * 2 + (half if e == 0 else 1 - half)
        return remote(cols_ref.at[to, rows], rows_ref.at[s, rows], send.at[n, e], recv.at[n, e], to, k)

    first_rows, last_rows = pl.ds(0, OWN), pl.ds(OWN, OWN)
    products, queries = [], []
    order = (4, 3, 5, 2, 6, 1, 7, 0)
    for n in order:
        there = (z + n) % Z
        short = [
            short_convolve(feat_ref, taps_ref, halo_in, agreement, g, there).astype(F32) for g in (1, 2)
        ]
        product = (short[0] * short[1]).astype(BF16).T
        for h in range(2):
            cols_ref[2 * there + h, 0:OWN, :] = product[h * OWN : (h + 1) * OWN]
        for e in range(2):
            if n or e:
                products.append(spread(n, e, first_rows, p_s, p_r))
                products[-1].start()
    for n in order:
        there = (z + n) % Z
        query = short_convolve(feat_ref, taps_ref, halo_in, agreement, 0, there).T
        for h in range(2):
            cols_ref[2 * there + h, OWN:B, :] = query[h * OWN : (h + 1) * OWN]
        for e in range(2):
            if n or e:
                queries.append(spread(n, e, last_rows, q_s, q_r))
                queries[-1].start()
    rows_ref[s] = cols_ref[s]
    build_toeplitz(filt_ref, toep_ref, 2, 8)

    emb_copy.wait()
    wanted = jnp.broadcast_to(ids_ref[...], (B, B)).T
    lane = lax.broadcasted_iota(jnp.int32, (B, B), 1)
    vocab = emb_ref.shape[0] // B
    hot = jnp.concatenate([(wanted == lane + v * B).astype(F32).astype(BF16) for v in range(vocab)], axis=1)
    for n in range(8):
        cols = slice(n * B, (n + 1) * B)
        look_ref[:, cols] = jnp.dot(hot, emb_ref[:, cols], preferred_element_type=F32).astype(BF16)
    skip = jnp.broadcast_to(skip_ref[...], (B, OWN)).T

    for copy in products:
        copy.wait()
    x_ref[0 : LAGS * PITCH, :] = jnp.zeros((LAGS * PITCH, B), F32)
    for i in range(SEQ):
        at = (LAGS + i) * PITCH
        x_ref[at : at + OWN, :] = rows_ref[i, 0:OWN, :].astype(F32)
    long_convolve(toep_ref, x_ref, y_ref, b1, b2)
    for copy in queries:
        copy.wait()
    mate = []
    for c in range(Z):
        for parity in range(2):
            i = 2 * (c // 2 + 4 * (c % 2)) + parity
            signal = rows_ref[i, 0:OWN, :].astype(F32)
            convolved = (y_ref[i * PITCH : i * PITCH + OWN, :] + skip * signal).astype(BF16)
            gated = rows_ref[i, OWN:B, :].astype(F32) * convolved.astype(F32)
            gated_ref[parity, c] = gated.astype(BF16)
        copy = remote(gated_ref.at[1 - half, c], pair_ref.at[c, half], y_s.at[c], y_r.at[c], mate_seq, k)
        copy.start()
        mate.append(copy)
    for c in range(Z):
        pair_ref[c, half] = gated_ref[half, c]

    w_copy.start()
    up_seq, down_seq = (z + 1) % Z * 2 + half, (z + Z - 1) % Z * 2 + half

    def up(c, n):
        block = g_ref.at[c, (z + Z - n + 1) % Z]
        return remote(block, block, up_s.at[c, n], up_r.at[c, n], up_seq, k)

    def down(c, n):
        block = g_ref.at[c, (z + n - 1) % Z]
        return remote(block, block, down_s.at[c, n], down_r.at[c, n], down_seq, k)

    def up_has(c, n):
        return n <= 3 + (c % 2 == 0)

    def down_has(c, n):
        return n <= 3 + (c % 2 == 1)

    def own(c):
        mate[c].wait_recv()
        g_ref[c, z] = pair_ref[c].reshape(B, B).T
        up(c, 1).start()
        down(c, 1).start()

    def forward(c, n):
        if up_has(c, n):
            up(c, n).wait_recv()
            if up_has(c, n + 1):
                up(c, n + 1).start()
        if down_has(c, n):
            down(c, n).wait_recv()
            if down_has(c, n + 1):
                down(c, n + 1).start()

    yl, x = k // 4, k % 4
    across = (1 - yl) * 4 + x

    def along(e):
        return yl * 4 + (x + e) % 4

    def first_y(j):
        return remote(part_y.at[j, pl.ds((1 - yl) * 4, 4)], got_y.at[j], ya_s.at[j], ya_r.at[j], s, across)

    def second_x(j, e):
        return remote(mid_y.at[j, e], end_y.at[j, e], yb_s.at[j, e], yb_r.at[j, e], s, along(e))

    def first_x(j, e):
        return remote(
            part_x.at[j, pl.ds((x + e) % 4 * 2, 2)], got_x.at[j, e], xa_s.at[j, e], xa_r.at[j, e], s, along(e)
        )

    def second_y(j):
        return remote(mid_x.at[j, 1 - yl], end_x.at[j], xb_s.at[j], xb_r.at[j], s, across)

    def project(j, turns):
        lhs = jnp.concatenate(
            [jnp.concatenate([g_ref[q, zz] for zz in range(Z)], axis=1) for q in (2 * j, 2 * j + 1)], axis=0
        )
        for e in turns:
            there = (x + e) % 4
            rhs = jnp.concatenate([w_ref[there], w_ref[4 + there]], axis=1)
            value = jnp.dot(lhs, rhs, preferred_element_type=F32).astype(BF16)
            for n in range(2):
                part_y[j, n * 4 + there] = value[0:B, n * B : (n + 1) * B]
                part_x[j, there * 2 + n] = value[B : 2 * B, n * B : (n + 1) * B]
            if e:
                first_x(j, e).start()
            else:
                first_y(j).start()

    def middle(j):
        first_y(j).wait_recv()
        for e in (2, 1, 3, 0):
            there = (x + e) % 4
            total = part_y[j, yl * 4 + there].astype(F32) + got_y[j, there].astype(F32)
            mid_y[j, e] = total.astype(BF16)
            if e:
                second_x(j, e).start()
        for e in (1, 2, 3):
            first_x(j, e).wait_recv()
        for n in range(2):
            total = part_x[j, x * 2 + n].astype(F32)
            for e in (1, 2, 3):
                total = total + got_x[j, e, n].astype(F32)
            mid_x[j, n] = total.astype(BF16)
        second_y(j).start()

    def to_plane(j, q):
        owner = j + 4 * q
        return owner, remote(sum_ref.at[j, q], plane_ref.at[z], z_s.at[j, q], z_r.at[z], owner * 2 + half, k)

    def collect(j):
        for q in range(2):
            if q == 0:
                total = mid_y[j, 0].astype(F32)
                for e in (1, 2, 3):
                    second_x(j, e).wait_recv()
                    total = total + end_y[j, e].astype(F32)
            else:
                second_y(j).wait_recv()
                total = mid_x[j, yl].astype(F32) + end_x[j].astype(F32)
            sum_ref[j, q] = total.astype(BF16)
            owner, copy = to_plane(j, q)

            @pl.when(z != owner)
            def _():
                copy.start()

            @pl.when(z == owner)
            def _():
                plane_ref[owner] = sum_ref[j, q]

    own(0)
    own(1)
    own(2)
    own(3)
    own(4)
    own(5)
    own(6)
    own(7)
    forward(0, 1)
    forward(1, 1)
    forward(2, 1)
    forward(3, 1)
    forward(4, 1)
    forward(5, 1)
    forward(6, 1)
    forward(7, 1)
    forward(0, 2)
    forward(1, 2)
    forward(2, 2)
    forward(3, 2)
    forward(4, 2)
    forward(5, 2)
    forward(6, 2)
    forward(7, 2)
    w_copy.wait_recv()
    w_share.start()
    forward(0, 3)
    forward(1, 3)
    forward(2, 3)
    forward(3, 3)
    forward(4, 3)
    forward(5, 3)
    forward(6, 3)
    forward(7, 3)
    forward(0, 4)
    forward(1, 4)
    w_share.wait_recv()
    project(0, (2, 1))
    forward(2, 4)
    forward(3, 4)
    project(0, (3, 0))
    forward(4, 4)
    forward(5, 4)
    project(1, (2, 1))
    forward(6, 4)
    forward(7, 4)
    project(1, (3, 0))
    project(2, (2, 1))
    project(2, (3, 0))
    project(3, (2, 1))
    project(3, (3, 0))
    middle(0)
    middle(1)
    middle(2)
    middle(3)
    collect(0)
    collect(1)
    collect(2)
    collect(3)
    for zz in range(Z):

        @pl.when(z != zz)
        def _():
            remote(sum_ref.at[0, 0], plane_ref.at[zz], z_s.at[0, 0], z_r.at[zz], zz * 2 + half, k).wait_recv()

        @pl.when(k != zz)
        def _():
            remote(plane_ref.at[zz], last_ref.at[k], f_s.at[zz], f_r.at[k], s, zz).start()

        @pl.when(k == zz)
        def _():
            last_ref[zz] = plane_ref[zz]

    for kk in range(CHAN):

        @pl.when(k != kk)
        def _():
            remote(plane_ref.at[0], last_ref.at[kk], f_s.at[0], f_r.at[kk], s, kk).wait_recv()

        cols = slice(kk * B, (kk + 1) * B)
        out_ref[:, cols] = (last_ref[kk].astype(F32) + look_ref[:, cols].astype(F32)).astype(BF16)

    for copy in mate:
        copy.wait_send()
    w_copy.wait_send()
    w_share.wait_send()
    for c in range(Z):
        for n in range(1, 5):
            if up_has(c, n):
                up(c, n).wait_send()
            if down_has(c, n):
                down(c, n).wait_send()
    for j in range(4):
        first_y(j).wait_send()
        second_y(j).wait_send()
        for e in (1, 2, 3):
            first_x(j, e).wait_send()
            second_x(j, e).wait_send()
    for j in range(4):
        for q in range(2):
            owner, copy = to_plane(j, q)

            @pl.when(z != owner)
            def _():
                copy.wait_send()

    for zz in range(Z):

        @pl.when(k != zz)
        def _():
            remote(plane_ref.at[zz], last_ref.at[k], f_s.at[zz], f_r.at[k], s, zz).wait_send()


def local(features, lengths, ids, taps, filters, skip, out_weight, embedding):
    vmem = pl.BlockSpec(memory_space=pltpu.VMEM)
    hbm = pl.BlockSpec(memory_space=pl.ANY)
    dma = pltpu.SemaphoreType.DMA
    tile = (B, B)
    return pl.pallas_call(
        kernel,
        out_shape=jax.ShapeDtypeStruct((B, CHAN * B), BF16),
        in_specs=[pl.BlockSpec(memory_space=pltpu.SMEM), vmem, vmem, vmem, vmem, hbm, vmem, hbm],
        out_specs=vmem,
        scratch_shapes=[
            pltpu.VMEM((16, CHAN * B), BF16),
            pltpu.VMEM((16, CHAN * B), BF16),
            pltpu.VMEM((SEQ,) + tile, BF16),
            pltpu.VMEM((SEQ,) + tile, BF16),
            pltpu.VMEM((OWN, (LAGS + 1) * B, B), BF16),
            pltpu.VMEM(((LAGS + SEQ) * PITCH, B), F32),
            pltpu.VMEM((SEQ * PITCH, B), F32),
            pltpu.VMEM((2, 8, OWN, B), BF16),
            pltpu.VMEM((8, 2, OWN, B), BF16),
            pltpu.VMEM((CHAN, CHAN * B, B), BF16),
            pltpu.VMEM(embedding.shape, BF16),
            pltpu.VMEM((8, Z) + tile, BF16),
            pltpu.VMEM((4, CHAN) + tile, BF16),
            pltpu.VMEM((4, CHAN) + tile, BF16),
            pltpu.VMEM((4, 4) + tile, BF16),
            pltpu.VMEM((4, 4, 2) + tile, BF16),
            pltpu.VMEM((4, 4) + tile, BF16),
            pltpu.VMEM((4, 2) + tile, BF16),
            pltpu.VMEM((4, 4) + tile, BF16),
            pltpu.VMEM((4,) + tile, BF16),
            pltpu.VMEM((4, 2) + tile, BF16),
            pltpu.VMEM((Z,) + tile, BF16),
            pltpu.VMEM((CHAN,) + tile, BF16),
            pltpu.VMEM((B, CHAN * B), BF16),
            dma((4,)), dma,
            dma, dma, dma, dma, dma, dma,
            dma((Z, 2)), dma((Z, 2)), dma((Z, 2)), dma((Z, 2)),
            dma((Z,)), dma((Z,)),
            dma((Z, 5)), dma((Z, 5)), dma((Z, 5)), dma((Z, 5)),
            dma((4,)), dma((4,)), dma((4, 4)), dma((4, 4)), dma((4, 4)), dma((4, 4)), dma((4,)), dma((4,)),
            dma((4, 2)), dma((Z,)),
            dma((Z,)), dma((CHAN,)),
        ],
        compiler_params=pltpu.CompilerParams(
            collective_id=0, has_side_effects=True, vmem_limit_bytes=56 * 2**20
        ),
        name="hyena_block",
    )(
        lengths,
        features.transpose(1, 0, 2),
        taps,
        filters,
        skip.reshape(1, -1),
        out_weight,
        ids.reshape(1, -1),
        embedding,
    )


def solution(mesh):
    placed = (
        P(("dp", "seq"), None, "chan"),
        P("dp"),
        P(("dp", "seq")),
        P(None, None, "chan"),
        P(("chan", "seq"), None),
        P(("chan", "seq")),
        P("chan", "seq"),
        P(None, "chan"),
    )
    return jax.shard_map(
        local, mesh=mesh, in_specs=placed, out_specs=P(("dp", "seq"), "chan"), check_vma=False
    )
```

```python
import jax
import jax.numpy as jnp
from jax import lax
from jax.experimental import pallas as pl
from jax.experimental.pallas import tpu as pltpu
from jax.sharding import PartitionSpec as P

MESH = pl.DeviceIdType.MESH
F32, BF16 = jnp.float32, jnp.bfloat16
B = 128
SEQ, CHAN, Z = 16, 8, 8
OWN = 64
LAGS = 8
PITCH = 65


def build_toeplitz(filt_ref, toep_ref, first, last):
    row = lax.broadcasted_iota(jnp.int32, (B, B), 0)
    col = lax.broadcasted_iota(jnp.int32, (B, B), 1)
    upper = col >= row

    def step(g, _):
        taps = filt_ref[pl.ds(pl.multiple_of(g * 8, 8), 8), :]
        for j in range(8):
            before = jnp.zeros((B, B), F32)
            for d in range(LAGS + 1):
                if d < LAGS:
                    line = jnp.broadcast_to(taps[j : j + 1, d * B : (d + 1) * B], (B, B))
                    now = pltpu.roll(line, 0, 1, stride=1, stride_axis=0)
                else:
                    now = jnp.zeros((B, B), F32)
                toep_ref[g * 8 + j, d * B : (d + 1) * B, :] = jnp.where(upper, now, before).astype(BF16)
                before = now
        return 0

    lax.fori_loop(first, last, step, 0)


def document(position, b1, b2):
    return (position >= b1).astype(jnp.int32) + (position >= b2).astype(jnp.int32)


def short_agreement(s, b1, b2):
    row = lax.broadcasted_iota(jnp.int32, (B, B), 0)
    position = s * B + row
    here = document(position, b1, b2)
    agree1 = ((document(position - 1, b1, b2) == here) & (position >= 1)).astype(F32)
    agree2 = ((document(position - 2, b1, b2) == here) & (position >= 2)).astype(F32)
    return row, agree1, agree2


def short_convolve(feat_ref, taps_ref, halo_ref, agreement, g, n):
    row, agree1, agree2 = agreement
    cols = pl.ds(pl.multiple_of(n * B, B), B)
    x = feat_ref[g, :, cols].astype(F32)
    halo = halo_ref[:, cols].astype(F32)
    older, newer = halo[2 * g : 2 * g + 1], halo[2 * g + 1 : 2 * g + 2]
    x1 = jnp.where(row < 1, newer, pltpu.roll(x, 1, 0))
    x2 = jnp.where(row < 1, older, jnp.where(row < 2, newer, pltpu.roll(x, 2, 0)))
    t = [taps_ref[lag, pl.ds(g, 1), cols] for lag in range(3)]
    return (t[0] * x + t[1] * x1 * agree1 + t[2] * x2 * agree2).astype(BF16)


def long_convolve(toep_ref, x_ref, y_ref, b1, b2):
    block = lax.broadcasted_iota(jnp.int32, (SEQ, B), 0)
    lane = lax.broadcasted_iota(jnp.int32, (SEQ, B), 1)

    def docs(d):
        return document((block - d) * B + lane, b1, b2)

    masks = [[(docs(d) == k).astype(F32).astype(BF16) for d in range(LAGS + 1)] for k in range(3)]
    here = docs(0)

    def step(c, _):
        lhs = []
        for d in range(LAGS + 1):
            x = x_ref[pl.ds((LAGS - d) * PITCH + c, SEQ, stride=PITCH), :].astype(BF16)
            lhs.append(jnp.concatenate([masks[k][d] * x for k in range(3)], axis=0))
        y = jnp.dot(jnp.concatenate(lhs, axis=1), toep_ref[c], preferred_element_type=F32)
        y_ref[pl.ds(c, SEQ, stride=PITCH), :] = jnp.where(
            here == 0, y[0:SEQ], jnp.where(here == 1, y[SEQ : 2 * SEQ], y[2 * SEQ : 3 * SEQ])
        )
        return 0

    lax.fori_loop(0, OWN, step, 0, unroll=8)


def kernel(
    len_ref, feat_hbm, taps_ref, filt_hbm, skip_ref, w_hbm, ids_ref, emb_hbm, out_ref,
    feat_ref, filt_ref, halo_out, halo_in, cols_ref, rows_ref, toep_ref, x_ref, y_ref, gated_ref, pair_ref, w_ref, emb_ref, g_ref,
    part_y, part_x, got_y, got_x, mid_y, mid_x, end_y, end_x, sum_ref, plane_ref, last_ref, look_ref,
    own_s, emb_s, feat_s, filt_s, halo_s, halo_r, w_s, w_r, sib_s, sib_r, p_s, p_r, q_s, q_r, y_s, y_r,
    up_s, up_r, down_s, down_r, ya_s, ya_r, yb_s, yb_r, xa_s, xa_r, xb_s, xb_r, z_s, z_r, f_s, f_r,
):
    dp = lax.axis_index("dp")
    s = lax.axis_index("seq")
    k = lax.axis_index("chan")
    z, half = s // 2, s % 2
    mate_seq = z * 2 + 1 - half

    barrier = pltpu.get_barrier_semaphore()
    for d in range(1, SEQ):
        pl.semaphore_signal(barrier, inc=1, device_id=(dp, (s + d) % SEQ, k), device_id_type=MESH)
    for d in range(1, CHAN):
        pl.semaphore_signal(barrier, inc=1, device_id=(dp, s, (k + d) % CHAN), device_id_type=MESH)
    pl.semaphore_signal(barrier, inc=1, device_id=(1 - dp, s, k), device_id_type=MESH)

    feat_copy = pltpu.make_async_copy(feat_hbm, feat_ref, feat_s)
    filt_copy = pltpu.make_async_copy(filt_hbm.at[:, pl.ds(0, LAGS * B)], filt_ref, filt_s)
    feat_copy.start()
    filt_copy.start()
    own_w = [
        pltpu.make_async_copy(w_hbm.at[:, pl.ds(b * B, B)], w_ref.at[half * 4 + b], own_s.at[b]) for b in range(4)
    ]
    emb_copy = pltpu.make_async_copy(emb_hbm, emb_ref, emb_s)
    for copy in own_w:
        copy.start()
    emb_copy.start()

    b1 = len_ref[0]
    b2 = b1 + len_ref[1]

    def remote(src, dst, send, recv, seq, chan, core=dp):
        return pltpu.make_async_remote_copy(
            src_ref=src, dst_ref=dst, send_sem=send, recv_sem=recv, device_id=(core, seq, chan), device_id_type=MESH
        )

    feat_copy.wait()
    edge = [feat_ref[g, B - 16 : B, :].astype(F32)[14:16] for g in range(3)]
    halo_out[...] = jnp.concatenate(edge + [jnp.zeros((10, CHAN * B), F32)], axis=0).astype(BF16)
    pl.semaphore_wait(barrier, SEQ - 1 + CHAN - 1 + 1)

    halo_copy = remote(halo_out, halo_in, halo_s, halo_r, (s + 1) % SEQ, k)
    halo_copy.start()
    depth = w_ref.shape[1] // 2

    def fetch(n):
        mine = w_ref.at[pl.ds(half * 4 + 2 * n, 2), pl.ds(dp * depth, depth)]
        return remote(mine, mine, w_s.at[n], w_r.at[n], mate_seq, k)

    def share(n):
        theirs = w_ref.at[pl.ds((1 - half) * 4 + 2 * n, 2), pl.ds(dp * depth, depth)]
        return remote(theirs, theirs, sib_s.at[n], sib_r.at[n], s, k, 1 - dp)

    for copy in own_w:
        copy.wait()
    fetch(0).start()
    filt_copy.wait()
    build_toeplitz(filt_ref, toep_ref, 0, 2)
    halo_copy.wait()
    agreement = short_agreement(s, b1, b2)

    def spread(n, e, rows, send, recv):
        to = (z + n) % Z * 2 + (half if e == 0 else 1 - half)
        return remote(cols_ref.at[to, rows], rows_ref.at[s, rows], send.at[n, e], recv.at[n, e], to, k)

    first_rows, last_rows = pl.ds(0, OWN), pl.ds(OWN, OWN)
    products, queries = [], []
    order = (4, 3, 5, 2, 6, 1, 7, 0)
    for n in order:
        there = (z + n) % Z
        short = [
            short_convolve(feat_ref, taps_ref, halo_in, agreement, g, there).astype(F32) for g in (1, 2)
        ]
        product = (short[0] * short[1]).astype(BF16).T
        for h in range(2):
            cols_ref[2 * there + h, 0:OWN, :] = product[h * OWN : (h + 1) * OWN]
        for e in range(2):
            if n or e:
                products.append(spread(n, e, first_rows, p_s, p_r))
                products[-1].start()
    for n in order:
        there = (z + n) % Z
        query = short_convolve(feat_ref, taps_ref, halo_in, agreement, 0, there).T
        for h in range(2):
            cols_ref[2 * there + h, OWN:B, :] = query[h * OWN : (h + 1) * OWN]
        for e in range(2):
            if n or e:
                queries.append(spread(n, e, last_rows, q_s, q_r))
                queries[-1].start()
    rows_ref[s] = cols_ref[s]
    build_toeplitz(filt_ref, toep_ref, 2, 8)

    emb_copy.wait()
    wanted = jnp.broadcast_to(ids_ref[...], (B, B)).T
    lane = lax.broadcasted_iota(jnp.int32, (B, B), 1)
    vocab = emb_ref.shape[0] // B
    hot = jnp.concatenate([(wanted == lane + v * B).astype(F32).astype(BF16) for v in range(vocab)], axis=1)
    for n in range(8):
        cols = slice(n * B, (n + 1) * B)
        look_ref[:, cols] = jnp.dot(hot, emb_ref[:, cols], preferred_element_type=F32).astype(BF16)
    skip = jnp.broadcast_to(skip_ref[...], (B, OWN)).T

    for copy in products:
        copy.wait()
    x_ref[0 : LAGS * PITCH, :] = jnp.zeros((LAGS * PITCH, B), F32)
    for i in range(SEQ):
        at = (LAGS + i) * PITCH
        x_ref[at : at + OWN, :] = rows_ref[i, 0:OWN, :].astype(F32)
    long_convolve(toep_ref, x_ref, y_ref, b1, b2)
    for copy in queries:
        copy.wait()
    mate = []
    for c in range(Z):
        for parity in range(2):
            i = 2 * (c // 2 + 4 * (c % 2)) + parity
            signal = rows_ref[i, 0:OWN, :].astype(F32)
            convolved = (y_ref[i * PITCH : i * PITCH + OWN, :] + skip * signal).astype(BF16)
            gated = rows_ref[i, OWN:B, :].astype(F32) * convolved.astype(F32)
            gated_ref[parity, c] = gated.astype(BF16)
        copy = remote(gated_ref.at[1 - half, c], pair_ref.at[c, half], y_s.at[c], y_r.at[c], mate_seq, k)
        copy.start()
        mate.append(copy)
    for c in range(Z):
        pair_ref[c, half] = gated_ref[half, c]

    fetch(1).start()
    fetch(0).wait_recv()
    share(0).start()
    up_seq, down_seq = (z + 1) % Z * 2 + half, (z + Z - 1) % Z * 2 + half

    def up(c, n):
        block = g_ref.at[pl.ds(2 * c, 2), (z + Z - n + 1) % Z]
        return remote(block, block, up_s.at[c, n], up_r.at[c, n], up_seq, k)

    def down(c, n):
        block = g_ref.at[pl.ds(2 * c, 2), (z + n - 1) % Z]
        return remote(block, block, down_s.at[c, n], down_r.at[c, n], down_seq, k)

    def up_has(c, n):
        return n <= 3 + (c % 2 == 0)

    def down_has(c, n):
        return n <= 3 + (c % 2 == 1)

    def own(c):
        for q in (2 * c, 2 * c + 1):
            mate[q].wait_recv()
            g_ref[q, z] = pair_ref[q].reshape(B, B).T
        up(c, 1).start()
        down(c, 1).start()

    def forward(c, n):
        if up_has(c, n):
            up(c, n).wait_recv()
            if up_has(c, n + 1):
                up(c, n + 1).start()
        if down_has(c, n):
            down(c, n).wait_recv()
            if down_has(c, n + 1):
                down(c, n + 1).start()

    yl, x = k // 4, k % 4
    across = (1 - yl) * 4 + x

    def along(e):
        return yl * 4 + (x + e) % 4

    def first_y(j):
        return remote(part_y.at[j, pl.ds((1 - yl) * 4, 4)], got_y.at[j], ya_s.at[j], ya_r.at[j], s, across)

    def second_x(j, e):
        return remote(mid_y.at[j, e], end_y.at[j, e], yb_s.at[j, e], yb_r.at[j, e], s, along(e))

    def first_x(j, e):
        return remote(
            part_x.at[j, pl.ds((x + e) % 4 * 2, 2)], got_x.at[j, e], xa_s.at[j, e], xa_r.at[j, e], s, along(e)
        )

    def second_y(j):
        return remote(mid_x.at[j, 1 - yl], end_x.at[j], xb_s.at[j], xb_r.at[j], s, across)

    def project(j, turns):
        lhs = jnp.concatenate(
            [jnp.concatenate([g_ref[q, zz] for zz in range(Z)], axis=1) for q in (2 * j, 2 * j + 1)], axis=0
        )
        for e in turns:
            there = (x + e) % 4
            rhs = jnp.concatenate([w_ref[there], w_ref[4 + there]], axis=1)
            value = jnp.dot(lhs, rhs, preferred_element_type=F32).astype(BF16)
            for n in range(2):
                part_y[j, n * 4 + there] = value[0:B, n * B : (n + 1) * B]
                part_x[j, there * 2 + n] = value[B : 2 * B, n * B : (n + 1) * B]
            if e:
                first_x(j, e).start()
            else:
                first_y(j).start()

    def middle(j):
        first_y(j).wait_recv()
        for e in (2, 1, 3, 0):
            there = (x + e) % 4
            total = part_y[j, yl * 4 + there].astype(F32) + got_y[j, there].astype(F32)
            mid_y[j, e] = total.astype(BF16)
            if e:
                second_x(j, e).start()
        for e in (1, 2, 3):
            first_x(j, e).wait_recv()
        for n in range(2):
            total = part_x[j, x * 2 + n].astype(F32)
            for e in (1, 2, 3):
                total = total + got_x[j, e, n].astype(F32)
            mid_x[j, n] = total.astype(BF16)
        second_y(j).start()

    def to_plane(j, q):
        owner = j + 4 * q
        return owner, remote(sum_ref.at[j, q], plane_ref.at[z], z_s.at[j, q], z_r.at[z], owner * 2 + half, k)

    def collect(j):
        for q in range(2):
            if q == 0:
                total = mid_y[j, 0].astype(F32)
                for e in (1, 2, 3):
                    second_x(j, e).wait_recv()
                    total = total + end_y[j, e].astype(F32)
            else:
                second_y(j).wait_recv()
                total = mid_x[j, yl].astype(F32) + end_x[j].astype(F32)
            sum_ref[j, q] = total.astype(BF16)
            owner, copy = to_plane(j, q)

            @pl.when(z != owner)
            def _():
                copy.start()

            @pl.when(z == owner)
            def _():
                plane_ref[owner] = sum_ref[j, q]

    own(0)
    own(1)
    own(2)
    own(3)
    forward(0, 1)
    forward(1, 1)
    forward(2, 1)
    forward(3, 1)
    forward(0, 2)
    forward(1, 2)
    forward(2, 2)
    forward(3, 2)
    fetch(1).wait_recv()
    share(1).start()
    forward(0, 3)
    forward(1, 3)
    forward(2, 3)
    forward(3, 3)
    forward(0, 4)
    share(0).wait_recv()
    share(1).wait_recv()
    project(0, (2, 1, 3, 0))
    forward(1, 4)
    project(1, (2, 1, 3, 0))
    forward(2, 4)
    project(2, (2, 1, 3, 0))
    forward(3, 4)
    project(3, (2, 1, 3, 0))
    middle(0)
    middle(1)
    middle(2)
    middle(3)
    collect(0)
    collect(1)
    collect(2)
    collect(3)

    for zz in range(Z):

        @pl.when(z != zz)
        def _():
            remote(sum_ref.at[0, 0], plane_ref.at[zz], z_s.at[0, 0], z_r.at[zz], zz * 2 + half, k).wait_recv()

        @pl.when(k != zz)
        def _():
            remote(plane_ref.at[zz], last_ref.at[k], f_s.at[zz], f_r.at[k], s, zz).start()

        @pl.when(k == zz)
        def _():
            last_ref[zz] = plane_ref[zz]

    for kk in range(CHAN):

        @pl.when(k != kk)
        def _():
            remote(plane_ref.at[0], last_ref.at[kk], f_s.at[0], f_r.at[kk], s, kk).wait_recv()

        cols = slice(kk * B, (kk + 1) * B)
        out_ref[:, cols] = (last_ref[kk].astype(F32) + look_ref[:, cols].astype(F32)).astype(BF16)

    for copy in mate:
        copy.wait_send()
    for n in range(2):
        fetch(n).wait_send()
        share(n).wait_send()
    for c in range(4):
        for n in range(1, 5):
            if up_has(c, n):
                up(c, n).wait_send()
            if down_has(c, n):
                down(c, n).wait_send()
    for j in range(4):
        first_y(j).wait_send()
        second_y(j).wait_send()
        for e in (1, 2, 3):
            first_x(j, e).wait_send()
            second_x(j, e).wait_send()
    for j in range(4):
        for q in range(2):
            owner, copy = to_plane(j, q)

            @pl.when(z != owner)
            def _():
                copy.wait_send()

    for zz in range(Z):

        @pl.when(k != zz)
        def _():
            remote(plane_ref.at[zz], last_ref.at[k], f_s.at[zz], f_r.at[k], s, zz).wait_send()


def local(features, lengths, ids, taps, filters, skip, out_weight, embedding):
    vmem = pl.BlockSpec(memory_space=pltpu.VMEM)
    hbm = pl.BlockSpec(memory_space=pl.ANY)
    dma = pltpu.SemaphoreType.DMA
    tile = (B, B)
    return pl.pallas_call(
        kernel,
        out_shape=jax.ShapeDtypeStruct((B, CHAN * B), BF16),
        in_specs=[pl.BlockSpec(memory_space=pltpu.SMEM), hbm, vmem, hbm, vmem, hbm, vmem, hbm],
        out_specs=vmem,
        scratch_shapes=[
            pltpu.VMEM((3, B, CHAN * B), BF16),
            pltpu.VMEM((OWN, LAGS * B), F32),
            pltpu.VMEM((16, CHAN * B), BF16),
            pltpu.VMEM((16, CHAN * B), BF16),
            pltpu.VMEM((SEQ,) + tile, BF16),
            pltpu.VMEM((SEQ,) + tile, BF16),
            pltpu.VMEM((OWN, (LAGS + 1) * B, B), BF16),
            pltpu.VMEM(((LAGS + SEQ) * PITCH, B), F32),
            pltpu.VMEM((SEQ * PITCH, B), F32),
            pltpu.VMEM((2, 8, OWN, B), BF16),
            pltpu.VMEM((8, 2, OWN, B), BF16),
            pltpu.VMEM((CHAN, CHAN * B, B), BF16),
            pltpu.VMEM(embedding.shape, BF16),
            pltpu.VMEM((8, Z) + tile, BF16),
            pltpu.VMEM((4, CHAN) + tile, BF16),
            pltpu.VMEM((4, CHAN) + tile, BF16),
            pltpu.VMEM((4, 4) + tile, BF16),
            pltpu.VMEM((4, 4, 2) + tile, BF16),
            pltpu.VMEM((4, 4) + tile, BF16),
            pltpu.VMEM((4, 2) + tile, BF16),
            pltpu.VMEM((4, 4) + tile, BF16),
            pltpu.VMEM((4,) + tile, BF16),
            pltpu.VMEM((4, 2) + tile, BF16),
            pltpu.VMEM((Z,) + tile, BF16),
            pltpu.VMEM((CHAN,) + tile, BF16),
            pltpu.VMEM((B, CHAN * B), BF16),
            dma((4,)), dma, dma, dma,
            dma, dma, dma((2,)), dma((2,)), dma((2,)), dma((2,)),
            dma((Z, 2)), dma((Z, 2)), dma((Z, 2)), dma((Z, 2)),
            dma((Z,)), dma((Z,)),
            dma((4, 5)), dma((4, 5)), dma((4, 5)), dma((4, 5)),
            dma((4,)), dma((4,)), dma((4, 4)), dma((4, 4)), dma((4, 4)), dma((4, 4)), dma((4,)), dma((4,)),
            dma((4, 2)), dma((Z,)),
            dma((Z,)), dma((CHAN,)),
        ],
        compiler_params=pltpu.CompilerParams(
            collective_id=0, has_side_effects=True, vmem_limit_bytes=56 * 2**20
        ),
        name="hyena_block",
    )(
        lengths,
        features.transpose(1, 0, 2),
        taps,
        filters,
        skip.reshape(1, -1),
        out_weight,
        ids.reshape(1, -1),
        embedding,
    )


def solution(mesh):
    placed = (
        P(("dp", "seq"), None, "chan"),
        P("dp"),
        P(("dp", "seq")),
        P(None, None, "chan"),
        P(("chan", "seq"), None),
        P(("chan", "seq")),
        P("chan", "seq"),
        P(None, "chan"),
    )
    return jax.shard_map(
        local, mesh=mesh, in_specs=placed, out_specs=P(("dp", "seq"), "chan"), check_vma=False
    )
```

```python
import jax
import jax.numpy as jnp
from jax import lax
from jax.experimental import pallas as pl
from jax.experimental.pallas import tpu as pltpu
from jax.sharding import PartitionSpec as P

MESH = pl.DeviceIdType.MESH
F32, BF16 = jnp.float32, jnp.bfloat16
B = 128
SEQ, CHAN, Z = 16, 8, 8
OWN = 64
LAGS = 8
PITCH = 65


def build_toeplitz(filt_ref, toep_ref, first, last):
    row = lax.broadcasted_iota(jnp.int32, (B, B), 0)
    col = lax.broadcasted_iota(jnp.int32, (B, B), 1)
    upper = col >= row

    def step(g, _):
        taps = filt_ref[pl.ds(pl.multiple_of(g * 8, 8), 8), :]
        for j in range(8):
            before = jnp.zeros((B, B), F32)
            for d in range(LAGS + 1):
                if d < LAGS:
                    line = jnp.broadcast_to(taps[j : j + 1, d * B : (d + 1) * B], (B, B))
                    now = pltpu.roll(line, 0, 1, stride=1, stride_axis=0)
                else:
                    now = jnp.zeros((B, B), F32)
                toep_ref[g * 8 + j, d * B : (d + 1) * B, :] = jnp.where(upper, now, before).astype(BF16)
                before = now
        return 0

    lax.fori_loop(first, last, step, 0)


def document(position, b1, b2):
    return (position >= b1).astype(jnp.int32) + (position >= b2).astype(jnp.int32)


def short_agreement(s, b1, b2):
    row = lax.broadcasted_iota(jnp.int32, (B, B), 0)
    position = s * B + row
    here = document(position, b1, b2)
    agree1 = ((document(position - 1, b1, b2) == here) & (position >= 1)).astype(F32)
    agree2 = ((document(position - 2, b1, b2) == here) & (position >= 2)).astype(F32)
    return row, agree1, agree2


def short_convolve(feat_ref, taps_ref, halo_ref, agreement, g, n):
    row, agree1, agree2 = agreement
    cols = pl.ds(pl.multiple_of(n * B, B), B)
    x = feat_ref[g, :, cols].astype(F32)
    halo = halo_ref[:, cols].astype(F32)
    older, newer = halo[2 * g : 2 * g + 1], halo[2 * g + 1 : 2 * g + 2]
    x1 = jnp.where(row < 1, newer, pltpu.roll(x, 1, 0))
    x2 = jnp.where(row < 1, older, jnp.where(row < 2, newer, pltpu.roll(x, 2, 0)))
    t = [taps_ref[lag, pl.ds(g, 1), cols] for lag in range(3)]
    return (t[0] * x + t[1] * x1 * agree1 + t[2] * x2 * agree2).astype(BF16)


def long_convolve(toep_ref, x_ref, y_ref, b1, b2):
    block = lax.broadcasted_iota(jnp.int32, (SEQ, B), 0)
    lane = lax.broadcasted_iota(jnp.int32, (SEQ, B), 1)

    def docs(d):
        return document((block - d) * B + lane, b1, b2)

    masks = [[(docs(d) == k).astype(F32).astype(BF16) for d in range(LAGS + 1)] for k in range(3)]
    here = docs(0)

    def step(c, _):
        lhs = []
        for d in range(LAGS + 1):
            x = x_ref[pl.ds((LAGS - d) * PITCH + c, SEQ, stride=PITCH), :].astype(BF16)
            lhs.append(jnp.concatenate([masks[k][d] * x for k in range(3)], axis=0))
        y = jnp.dot(jnp.concatenate(lhs, axis=1), toep_ref[c], preferred_element_type=F32)
        y_ref[pl.ds(c, SEQ, stride=PITCH), :] = jnp.where(
            here == 0, y[0:SEQ], jnp.where(here == 1, y[SEQ : 2 * SEQ], y[2 * SEQ : 3 * SEQ])
        )
        return 0

    lax.fori_loop(0, OWN, step, 0, unroll=8)


def kernel(
    len_ref, feat_hbm, taps_ref, filt_hbm, skip_ref, w_hbm, ids_ref, emb_hbm, out_ref,
    feat_ref, filt_ref, halo_out, halo_in, cols_ref, rows_ref, toep_ref, x_ref, y_ref, gated_ref, pair_ref, w_ref, emb_ref, g_ref,
    part_y, part_x, got_y, got_x, mid_y, mid_x, end_y, end_x, sum_ref, plane_ref, last_ref, look_ref,
    own_s, emb_s, feat_s, filt_s, halo_s, halo_r, w_s, w_r, sib_s, sib_r, p_s, p_r, q_s, q_r, y_s, y_r,
    up_s, up_r, down_s, down_r, ya_s, ya_r, yb_s, yb_r, xa_s, xa_r, xb_s, xb_r, z_s, z_r, f_s, f_r,
):
    dp = lax.axis_index("dp")
    s = lax.axis_index("seq")
    k = lax.axis_index("chan")
    z, half = s // 2, s % 2
    mate_seq = z * 2 + 1 - half

    barrier = pltpu.get_barrier_semaphore()
    for d in range(1, SEQ):
        pl.semaphore_signal(barrier, inc=1, device_id=(dp, (s + d) % SEQ, k), device_id_type=MESH)
    for d in range(1, CHAN):
        pl.semaphore_signal(barrier, inc=1, device_id=(dp, s, (k + d) % CHAN), device_id_type=MESH)
    pl.semaphore_signal(barrier, inc=1, device_id=(1 - dp, s, k), device_id_type=MESH)

    feat_copy = pltpu.make_async_copy(feat_hbm, feat_ref, feat_s)
    filt_copy = pltpu.make_async_copy(filt_hbm.at[:, pl.ds(0, LAGS * B)], filt_ref, filt_s)
    feat_copy.start()
    filt_copy.start()
    own_w = [
        pltpu.make_async_copy(w_hbm.at[:, pl.ds(b * B, B)], w_ref.at[half * 4 + b], own_s.at[b]) for b in range(4)
    ]
    emb_copy = pltpu.make_async_copy(emb_hbm, emb_ref, emb_s)
    for copy in own_w:
        copy.start()
    emb_copy.start()

    b1 = len_ref[0]
    b2 = b1 + len_ref[1]

    def remote(src, dst, send, recv, seq, chan, core=dp):
        return pltpu.make_async_remote_copy(
            src_ref=src, dst_ref=dst, send_sem=send, recv_sem=recv, device_id=(core, seq, chan), device_id_type=MESH
        )

    feat_copy.wait()
    edge = [feat_ref[g, B - 16 : B, :].astype(F32)[14:16] for g in range(3)]
    halo_out[...] = jnp.concatenate(edge + [jnp.zeros((10, CHAN * B), F32)], axis=0).astype(BF16)
    pl.semaphore_wait(barrier, SEQ - 1 + CHAN - 1 + 1)

    halo_copy = remote(halo_out, halo_in, halo_s, halo_r, (s + 1) % SEQ, k)
    halo_copy.start()
    depth = w_ref.shape[1] // 2

    def fetch(n):
        mine = w_ref.at[pl.ds(half * 4 + 2 * n, 2), pl.ds(dp * depth, depth)]
        return remote(mine, mine, w_s.at[n], w_r.at[n], mate_seq, k)

    def share(n):
        theirs = w_ref.at[pl.ds((1 - half) * 4 + 2 * n, 2), pl.ds(dp * depth, depth)]
        return remote(theirs, theirs, sib_s.at[n], sib_r.at[n], s, k, 1 - dp)

    for copy in own_w:
        copy.wait()
    fetch(0).start()
    filt_copy.wait()
    build_toeplitz(filt_ref, toep_ref, 0, 2)
    halo_copy.wait()
    agreement = short_agreement(s, b1, b2)

    def spread(n, e, rows, send, recv):
        to = (z + n) % Z * 2 + (half if e == 0 else 1 - half)
        return remote(cols_ref.at[to, rows], rows_ref.at[s, rows], send.at[n, e], recv.at[n, e], to, k)

    first_rows, last_rows = pl.ds(0, OWN), pl.ds(OWN, OWN)
    products, queries = [], []
    order = (4, 3, 5, 2, 6, 1, 7, 0)
    for n in order:
        there = (z + n) % Z
        short = [
            short_convolve(feat_ref, taps_ref, halo_in, agreement, g, there).astype(F32) for g in (1, 2)
        ]
        product = (short[0] * short[1]).astype(BF16).T
        for h in range(2):
            cols_ref[2 * there + h, 0:OWN, :] = product[h * OWN : (h + 1) * OWN]
        for e in range(2):
            if n or e:
                products.append(spread(n, e, first_rows, p_s, p_r))
                products[-1].start()
    for n in order:
        there = (z + n) % Z
        query = short_convolve(feat_ref, taps_ref, halo_in, agreement, 0, there).T
        for h in range(2):
            cols_ref[2 * there + h, OWN:B, :] = query[h * OWN : (h + 1) * OWN]
        for e in range(2):
            if n or e:
                queries.append(spread(n, e, last_rows, q_s, q_r))
                queries[-1].start()
    rows_ref[s] = cols_ref[s]
    build_toeplitz(filt_ref, toep_ref, 2, 8)

    emb_copy.wait()
    wanted = jnp.broadcast_to(ids_ref[...], (B, B)).T
    lane = lax.broadcasted_iota(jnp.int32, (B, B), 1)
    vocab = emb_ref.shape[0] // B
    hot = jnp.concatenate([(wanted == lane + v * B).astype(F32).astype(BF16) for v in range(vocab)], axis=1)
    for n in range(8):
        cols = slice(n * B, (n + 1) * B)
        look_ref[:, cols] = jnp.dot(hot, emb_ref[:, cols], preferred_element_type=F32).astype(BF16)
    skip = jnp.broadcast_to(skip_ref[...], (B, OWN)).T

    for copy in products:
        copy.wait()
    x_ref[0 : LAGS * PITCH, :] = jnp.zeros((LAGS * PITCH, B), F32)
    for i in range(SEQ):
        at = (LAGS + i) * PITCH
        x_ref[at : at + OWN, :] = rows_ref[i, 0:OWN, :].astype(F32)
    long_convolve(toep_ref, x_ref, y_ref, b1, b2)
    for copy in queries:
        copy.wait()
    mate = []
    for c in range(Z):
        for parity in range(2):
            i = 2 * (c // 2 + 4 * (c % 2)) + parity
            signal = rows_ref[i, 0:OWN, :].astype(F32)
            convolved = (y_ref[i * PITCH : i * PITCH + OWN, :] + skip * signal).astype(BF16)
            gated = rows_ref[i, OWN:B, :].astype(F32) * convolved.astype(F32)
            gated_ref[parity, c] = gated.astype(BF16)
        copy = remote(gated_ref.at[1 - half, c], pair_ref.at[c, half], y_s.at[c], y_r.at[c], mate_seq, k)
        copy.start()
        mate.append(copy)
    for c in range(Z):
        pair_ref[c, half] = gated_ref[half, c]

    fetch(1).start()
    fetch(0).wait_recv()
    share(0).start()
    up_seq, down_seq = (z + 1) % Z * 2 + half, (z + Z - 1) % Z * 2 + half

    def up(c, n):
        block = g_ref.at[pl.ds(2 * c, 2), (z + Z - n + 1) % Z]
        return remote(block, block, up_s.at[c, n], up_r.at[c, n], up_seq, k)

    def down(c, n):
        block = g_ref.at[pl.ds(2 * c, 2), (z + n - 1) % Z]
        return remote(block, block, down_s.at[c, n], down_r.at[c, n], down_seq, k)

    def up_has(c, n):
        return n <= 3 + (c % 2 == 0)

    def down_has(c, n):
        return n <= 3 + (c % 2 == 1)

    def own(c):
        for q in (2 * c, 2 * c + 1):
            mate[q].wait_recv()
            g_ref[q, z] = pair_ref[q].reshape(B, B).T
        up(c, 1).start()
        down(c, 1).start()

    def forward(c, n):
        if up_has(c, n):
            up(c, n).wait_recv()
            if up_has(c, n + 1):
                up(c, n + 1).start()
        if down_has(c, n):
            down(c, n).wait_recv()
            if down_has(c, n + 1):
                down(c, n + 1).start()

    yl, x = k // 4, k % 4
    across = (1 - yl) * 4 + x

    def along(e):
        return yl * 4 + (x + e) % 4

    def first_y(j):
        return remote(part_y.at[j, pl.ds((1 - yl) * 4, 4)], got_y.at[j], ya_s.at[j], ya_r.at[j], s, across)

    def second_x(j, e):
        return remote(mid_y.at[j, e], end_y.at[j, e], yb_s.at[j, e], yb_r.at[j, e], s, along(e))

    def first_x(j, e):
        return remote(
            part_x.at[j, pl.ds((x + e) % 4 * 2, 2)], got_x.at[j, e], xa_s.at[j, e], xa_r.at[j, e], s, along(e)
        )

    def second_y(j):
        return remote(mid_x.at[j, 1 - yl], end_x.at[j], xb_s.at[j], xb_r.at[j], s, across)

    def project(j, turns):
        lhs = jnp.concatenate(
            [jnp.concatenate([g_ref[q, zz] for zz in range(Z)], axis=1) for q in (2 * j, 2 * j + 1)], axis=0
        )
        for e in turns:
            there = (x + e) % 4
            rhs = jnp.concatenate([w_ref[there], w_ref[4 + there]], axis=1)
            value = jnp.dot(lhs, rhs, preferred_element_type=F32).astype(BF16)
            for n in range(2):
                part_y[j, n * 4 + there] = value[0:B, n * B : (n + 1) * B]
                part_x[j, there * 2 + n] = value[B : 2 * B, n * B : (n + 1) * B]
            if e:
                first_x(j, e).start()
            else:
                first_y(j).start()

    def middle(j):
        first_y(j).wait_recv()
        for e in (2, 1, 3, 0):
            there = (x + e) % 4
            total = part_y[j, yl * 4 + there].astype(F32) + got_y[j, there].astype(F32)
            mid_y[j, e] = total.astype(BF16)
            if e:
                second_x(j, e).start()
        for e in (1, 2, 3):
            first_x(j, e).wait_recv()
        for n in range(2):
            total = part_x[j, x * 2 + n].astype(F32)
            for e in (1, 2, 3):
                total = total + got_x[j, e, n].astype(F32)
            mid_x[j, n] = total.astype(BF16)
        second_y(j).start()

    def to_plane(j, q):
        owner = j + 4 * q
        return owner, remote(sum_ref.at[j, q], plane_ref.at[z], z_s.at[j, q], z_r.at[z], owner * 2 + half, k)

    def collect(j):
        for q in range(2):
            if q == 0:
                total = mid_y[j, 0].astype(F32)
                for e in (1, 2, 3):
                    second_x(j, e).wait_recv()
                    total = total + end_y[j, e].astype(F32)
            else:
                second_y(j).wait_recv()
                total = mid_x[j, yl].astype(F32) + end_x[j].astype(F32)
            sum_ref[j, q] = total.astype(BF16)
            owner, copy = to_plane(j, q)

            @pl.when(z != owner)
            def _():
                copy.start()

            @pl.when(z == owner)
            def _():
                plane_ref[owner] = sum_ref[j, q]

    own(0)
    own(1)
    own(2)
    own(3)
    forward(0, 1)
    forward(1, 1)
    forward(2, 1)
    forward(3, 1)
    forward(0, 2)
    forward(1, 2)
    forward(2, 2)
    forward(3, 2)
    fetch(1).wait_recv()
    share(1).start()
    forward(0, 3)
    forward(1, 3)
    forward(2, 3)
    forward(3, 3)
    forward(0, 4)
    share(0).wait_recv()
    share(1).wait_recv()
    project(0, (2, 1, 3, 0))
    forward(1, 4)
    project(1, (2, 1, 3, 0))
    forward(2, 4)
    project(2, (2, 1, 3, 0))
    forward(3, 4)
    project(3, (2, 1, 3, 0))
    middle(0)
    middle(1)
    middle(2)
    middle(3)
    collect(0)
    collect(1)
    collect(2)
    collect(3)

    for zz in range(Z):

        @pl.when(z != zz)
        def _():
            remote(sum_ref.at[0, 0], plane_ref.at[zz], z_s.at[0, 0], z_r.at[zz], zz * 2 + half, k).wait_recv()

        @pl.when(k != zz)
        def _():
            remote(plane_ref.at[zz], last_ref.at[k], f_s.at[zz], f_r.at[k], s, zz).start()

        @pl.when(k == zz)
        def _():
            last_ref[zz] = plane_ref[zz]

    for kk in range(CHAN):

        @pl.when(k != kk)
        def _():
            remote(plane_ref.at[0], last_ref.at[kk], f_s.at[0], f_r.at[kk], s, kk).wait_recv()

        cols = slice(kk * B, (kk + 1) * B)
        out_ref[:, cols] = (last_ref[kk].astype(F32) + look_ref[:, cols].astype(F32)).astype(BF16)

    for copy in mate:
        copy.wait_send()
    for n in range(2):
        fetch(n).wait_send()
        share(n).wait_send()
    for c in range(4):
        for n in range(1, 5):
            if up_has(c, n):
                up(c, n).wait_send()
            if down_has(c, n):
                down(c, n).wait_send()
    for j in range(4):
        first_y(j).wait_send()
        second_y(j).wait_send()
        for e in (1, 2, 3):
            first_x(j, e).wait_send()
            second_x(j, e).wait_send()
    for j in range(4):
        for q in range(2):
            owner, copy = to_plane(j, q)

            @pl.when(z != owner)
            def _():
                copy.wait_send()

    for zz in range(Z):

        @pl.when(k != zz)
        def _():
            remote(plane_ref.at[zz], last_ref.at[k], f_s.at[zz], f_r.at[k], s, zz).wait_send()


def local(features, lengths, ids, taps, filters, skip, out_weight, embedding):
    vmem = pl.BlockSpec(memory_space=pltpu.VMEM)
    hbm = pl.BlockSpec(memory_space=pl.ANY)
    dma = pltpu.SemaphoreType.DMA
    tile = (B, B)
    return pl.pallas_call(
        kernel,
        out_shape=jax.ShapeDtypeStruct((B, CHAN * B), BF16),
        in_specs=[pl.BlockSpec(memory_space=pltpu.SMEM), hbm, vmem, hbm, vmem, hbm, vmem, hbm],
        out_specs=vmem,
        scratch_shapes=[
            pltpu.VMEM((3, B, CHAN * B), BF16),
            pltpu.VMEM((OWN, LAGS * B), F32),
            pltpu.VMEM((16, CHAN * B), BF16),
            pltpu.VMEM((16, CHAN * B), BF16),
            pltpu.VMEM((SEQ,) + tile, BF16),
            pltpu.VMEM((SEQ,) + tile, BF16),
            pltpu.VMEM((OWN, (LAGS + 1) * B, B), BF16),
            pltpu.VMEM(((LAGS + SEQ + 1) * PITCH, B), F32),
            pltpu.VMEM(((SEQ + 1) * PITCH, B), F32),
            pltpu.VMEM((2, 8, OWN, B), BF16),
            pltpu.VMEM((8, 2, OWN, B), BF16),
            pltpu.VMEM((CHAN, CHAN * B, B), BF16),
            pltpu.VMEM(embedding.shape, BF16),
            pltpu.VMEM((8, Z) + tile, BF16),
            pltpu.VMEM((4, CHAN) + tile, BF16),
            pltpu.VMEM((4, CHAN) + tile, BF16),
            pltpu.VMEM((4, 4) + tile, BF16),
            pltpu.VMEM((4, 4, 2) + tile, BF16),
            pltpu.VMEM((4, 4) + tile, BF16),
            pltpu.VMEM((4, 2) + tile, BF16),
            pltpu.VMEM((4, 4) + tile, BF16),
            pltpu.VMEM((4,) + tile, BF16),
            pltpu.VMEM((4, 2) + tile, BF16),
            pltpu.VMEM((Z,) + tile, BF16),
            pltpu.VMEM((CHAN,) + tile, BF16),
            pltpu.VMEM((B, CHAN * B), BF16),
            dma((4,)), dma, dma, dma,
            dma, dma, dma((2,)), dma((2,)), dma((2,)), dma((2,)),
            dma((Z, 2)), dma((Z, 2)), dma((Z, 2)), dma((Z, 2)),
            dma((Z,)), dma((Z,)),
            dma((4, 5)), dma((4, 5)), dma((4, 5)), dma((4, 5)),
            dma((4,)), dma((4,)), dma((4, 4)), dma((4, 4)), dma((4, 4)), dma((4, 4)), dma((4,)), dma((4,)),
            dma((4, 2)), dma((Z,)),
            dma((Z,)), dma((CHAN,)),
        ],
        compiler_params=pltpu.CompilerParams(
            collective_id=0, has_side_effects=True, vmem_limit_bytes=56 * 2**20
        ),
        name="hyena_block",
    )(
        lengths,
        features.transpose(1, 0, 2),
        taps,
        filters,
        skip.reshape(1, -1),
        out_weight,
        ids.reshape(1, -1),
        embedding,
    )


def solution(mesh):
    placed = (
        P(("dp", "seq"), None, "chan"),
        P("dp"),
        P(("dp", "seq")),
        P(None, None, "chan"),
        P(("chan", "seq"), None),
        P(("chan", "seq")),
        P("chan", "seq"),
        P(None, "chan"),
    )
    return jax.shard_map(
        local, mesh=mesh, in_specs=placed, out_specs=P(("dp", "seq"), "chan"), check_vma=False
    )
```

```python
import jax
import jax.numpy as jnp
from jax import lax
from jax.experimental import pallas as pl
from jax.experimental.pallas import tpu as pltpu
from jax.sharding import PartitionSpec as P

MESH = pl.DeviceIdType.MESH
F32, BF16 = jnp.float32, jnp.bfloat16
B = 128
SEQ, CHAN, Z = 16, 8, 8
OWN = 64
LAGS = 8
PITCH = 65


def build_toeplitz(filt_ref, toep_ref, first, last):
    row = lax.broadcasted_iota(jnp.int32, (B, B), 0)
    col = lax.broadcasted_iota(jnp.int32, (B, B), 1)
    upper = col >= row

    def step(g, _):
        taps = filt_ref[pl.ds(pl.multiple_of(g * 8, 8), 8), :]
        for j in range(8):
            before = jnp.zeros((B, B), F32)
            for d in range(LAGS + 1):
                if d < LAGS:
                    line = jnp.broadcast_to(taps[j : j + 1, d * B : (d + 1) * B], (B, B))
                    now = pltpu.roll(line, 0, 1, stride=1, stride_axis=0)
                else:
                    now = jnp.zeros((B, B), F32)
                toep_ref[g * 8 + j, d * B : (d + 1) * B, :] = jnp.where(upper, now, before).astype(BF16)
                before = now
        return 0

    lax.fori_loop(first, last, step, 0)


def document(position, b1, b2):
    return (position >= b1).astype(jnp.int32) + (position >= b2).astype(jnp.int32)


def short_agreement(s, b1, b2):
    row = lax.broadcasted_iota(jnp.int32, (B, B), 0)
    position = s * B + row
    here = document(position, b1, b2)
    agree1 = ((document(position - 1, b1, b2) == here) & (position >= 1)).astype(F32)
    agree2 = ((document(position - 2, b1, b2) == here) & (position >= 2)).astype(F32)
    return row, agree1, agree2


def short_convolve(feat_ref, taps_ref, halo_ref, agreement, g, n):
    row, agree1, agree2 = agreement
    cols = pl.ds(pl.multiple_of(n * B, B), B)
    x = feat_ref[g, :, cols].astype(F32)
    halo = halo_ref[:, cols].astype(F32)
    older, newer = halo[2 * g : 2 * g + 1], halo[2 * g + 1 : 2 * g + 2]
    x1 = jnp.where(row < 1, newer, pltpu.roll(x, 1, 0))
    x2 = jnp.where(row < 1, older, jnp.where(row < 2, newer, pltpu.roll(x, 2, 0)))
    t = [taps_ref[lag, pl.ds(g, 1), cols] for lag in range(3)]
    return (t[0] * x + t[1] * x1 * agree1 + t[2] * x2 * agree2).astype(BF16)


def long_convolve(toep_ref, x_ref, y_ref, b1, b2):
    block = lax.broadcasted_iota(jnp.int32, (SEQ, B), 0)
    lane = lax.broadcasted_iota(jnp.int32, (SEQ, B), 1)

    def docs(d):
        return document((block - d) * B + lane, b1, b2)

    masks = [[(docs(d) == k).astype(F32).astype(BF16) for d in range(LAGS + 1)] for k in range(3)]
    here = docs(0)

    def step(c, _):
        lhs = []
        for d in range(LAGS + 1):
            x = x_ref[pl.ds((LAGS - d) * PITCH + c, SEQ, stride=PITCH), :].astype(BF16)
            lhs.append(jnp.concatenate([masks[k][d] * x for k in range(3)], axis=0))
        y = jnp.dot(jnp.concatenate(lhs, axis=1), toep_ref[c], preferred_element_type=F32)
        y_ref[pl.ds(c, SEQ, stride=PITCH), :] = jnp.where(
            here == 0, y[0:SEQ], jnp.where(here == 1, y[SEQ : 2 * SEQ], y[2 * SEQ : 3 * SEQ])
        )
        return 0

    lax.fori_loop(0, OWN, step, 0, unroll=8)


def kernel(
    len_ref, feat_hbm, taps_ref, filt_hbm, skip_ref, w_hbm, ids_ref, emb_hbm, out_ref,
    feat_ref, filt_ref, halo_out, halo_in, cols_ref, rows_ref, toep_ref, x_ref, y_ref, gated_ref, pair_ref, w_ref, emb_ref, g_ref,
    part_y, part_x, got_y, got_x, mid_y, mid_x, end_y, end_x, sum_ref, plane_ref, last_ref, look_ref,
    own_s, emb_s, feat_s, filt_s, halo_s, halo_r, w_s, w_r, sib_s, sib_r, p_s, p_r, q_s, q_r, y_s, y_r,
    up_s, up_r, down_s, down_r, ya_s, ya_r, yb_s, yb_r, xa_s, xa_r, xb_s, xb_r, z_s, z_r, f_s, f_r,
):
    dp = lax.axis_index("dp")
    s = lax.axis_index("seq")
    k = lax.axis_index("chan")
    z, half = s // 2, s % 2
    mate_seq = z * 2 + 1 - half

    barrier = pltpu.get_barrier_semaphore()
    for d in range(1, SEQ):
        pl.semaphore_signal(barrier, inc=1, device_id=(dp, (s + d) % SEQ, k), device_id_type=MESH)
    for d in range(1, CHAN):
        pl.semaphore_signal(barrier, inc=1, device_id=(dp, s, (k + d) % CHAN), device_id_type=MESH)
    pl.semaphore_signal(barrier, inc=1, device_id=(1 - dp, s, k), device_id_type=MESH)

    feat_copy = pltpu.make_async_copy(feat_hbm, feat_ref, feat_s)
    filt_copy = pltpu.make_async_copy(filt_hbm.at[:, pl.ds(0, LAGS * B)], filt_ref, filt_s)
    feat_copy.start()
    filt_copy.start()
    own_w = [
        pltpu.make_async_copy(w_hbm.at[:, pl.ds(b * B, B)], w_ref.at[half * 4 + b], own_s.at[b]) for b in range(4)
    ]
    emb_copy = pltpu.make_async_copy(emb_hbm, emb_ref, emb_s)
    for copy in own_w:
        copy.start()
    emb_copy.start()

    b1 = len_ref[0]
    b2 = b1 + len_ref[1]

    def remote(src, dst, send, recv, seq, chan, core=dp):
        return pltpu.make_async_remote_copy(
            src_ref=src, dst_ref=dst, send_sem=send, recv_sem=recv, device_id=(core, seq, chan), device_id_type=MESH
        )

    feat_copy.wait()
    edge = [feat_ref[g, B - 16 : B, :].astype(F32)[14:16] for g in range(3)]
    halo_out[...] = jnp.concatenate(edge + [jnp.zeros((10, CHAN * B), F32)], axis=0).astype(BF16)
    pl.semaphore_wait(barrier, SEQ - 1 + CHAN - 1 + 1)

    halo_copy = remote(halo_out, halo_in, halo_s, halo_r, (s + 1) % SEQ, k)
    halo_copy.start()
    depth = w_ref.shape[1] // 2

    def fetch(n):
        mine = w_ref.at[pl.ds(half * 4 + 2 * n, 2), pl.ds(dp * depth, depth)]
        return remote(mine, mine, w_s.at[n], w_r.at[n], mate_seq, k)

    def share(n):
        theirs = w_ref.at[pl.ds((1 - half) * 4 + 2 * n, 2), pl.ds(dp * depth, depth)]
        return remote(theirs, theirs, sib_s.at[n], sib_r.at[n], s, k, 1 - dp)

    for copy in own_w:
        copy.wait()
    fetch(0).start()
    filt_copy.wait()
    build_toeplitz(filt_ref, toep_ref, 0, 2)
    halo_copy.wait()
    agreement = short_agreement(s, b1, b2)

    def spread(n, e, rows, send, recv):
        to = (z + n) % Z * 2 + (half if e == 0 else 1 - half)
        return remote(cols_ref.at[to, rows], rows_ref.at[s, rows], send.at[n, e], recv.at[n, e], to, k)

    first_rows, last_rows = pl.ds(0, OWN), pl.ds(OWN, OWN)
    products, queries = [], []
    order = (4, 3, 5, 2, 6, 1, 7, 0)
    for n in order:
        there = (z + n) % Z
        short = [
            short_convolve(feat_ref, taps_ref, halo_in, agreement, g, there).astype(F32) for g in (1, 2)
        ]
        product = (short[0] * short[1]).astype(BF16).T
        for h in range(2):
            cols_ref[2 * there + h, 0:OWN, :] = product[h * OWN : (h + 1) * OWN]
        for e in range(2):
            if n or e:
                products.append(spread(n, e, first_rows, p_s, p_r))
                products[-1].start()
    for n in order:
        there = (z + n) % Z
        query = short_convolve(feat_ref, taps_ref, halo_in, agreement, 0, there).T
        for h in range(2):
            cols_ref[2 * there + h, OWN:B, :] = query[h * OWN : (h + 1) * OWN]
        for e in range(2):
            if n or e:
                queries.append(spread(n, e, last_rows, q_s, q_r))
                queries[-1].start()
    rows_ref[s] = cols_ref[s]
    build_toeplitz(filt_ref, toep_ref, 2, 8)

    emb_copy.wait()
    wanted = jnp.broadcast_to(ids_ref[...], (B, B)).T
    lane = lax.broadcasted_iota(jnp.int32, (B, B), 1)
    vocab = emb_ref.shape[0] // B
    hot = jnp.concatenate([(wanted == lane + v * B).astype(F32).astype(BF16) for v in range(vocab)], axis=1)
    for n in range(8):
        cols = slice(n * B, (n + 1) * B)
        look_ref[:, cols] = jnp.dot(hot, emb_ref[:, cols], preferred_element_type=F32).astype(BF16)
    skip = jnp.broadcast_to(skip_ref[...], (B, OWN)).T

    for copy in products:
        copy.wait()
    x_ref[0 : LAGS * PITCH, :] = jnp.zeros((LAGS * PITCH, B), F32)
    for i in range(SEQ):
        at = (LAGS + i) * PITCH
        x_ref[at : at + OWN, :] = rows_ref[i, 0:OWN, :].astype(F32)
    long_convolve(toep_ref, x_ref, y_ref, b1, b2)
    for copy in queries:
        copy.wait()
    mate = []
    for c in range(Z):
        for parity in range(2):
            i = 2 * (c // 2 + 4 * (c % 2)) + parity
            signal = rows_ref[i, 0:OWN, :].astype(F32)
            convolved = (y_ref[i * PITCH : i * PITCH + OWN, :] + skip * signal).astype(BF16)
            gated = rows_ref[i, OWN:B, :].astype(F32) * convolved.astype(F32)
            gated_ref[parity, c] = gated.astype(BF16)
        copy = remote(gated_ref.at[1 - half, c], pair_ref.at[c, half], y_s.at[c], y_r.at[c], mate_seq, k)
        copy.start()
        mate.append(copy)
    for c in range(Z):
        pair_ref[c, half] = gated_ref[half, c]

    up_seq, down_seq = (z + 1) % Z * 2 + half, (z + Z - 1) % Z * 2 + half

    def up(c, n):
        block = g_ref.at[pl.ds(2 * c, 2), (z + Z - n + 1) % Z]
        return remote(block, block, up_s.at[c, n], up_r.at[c, n], up_seq, k)

    def down(c, n):
        block = g_ref.at[pl.ds(2 * c, 2), (z + n - 1) % Z]
        return remote(block, block, down_s.at[c, n], down_r.at[c, n], down_seq, k)

    def up_has(c, n):
        return n <= 3 + (c % 2 == 0)

    def down_has(c, n):
        return n <= 3 + (c % 2 == 1)

    def own(c):
        for q in (2 * c, 2 * c + 1):
            mate[q].wait_recv()
            g_ref[q, z] = pair_ref[q].reshape(B, B).T
        up(c, 1).start()
        down(c, 1).start()

    def forward(c, n):
        if up_has(c, n):
            up(c, n).wait_recv()
            if up_has(c, n + 1):
                up(c, n + 1).start()
        if down_has(c, n):
            down(c, n).wait_recv()
            if down_has(c, n + 1):
                down(c, n + 1).start()

    yl, x = k // 4, k % 4
    across = (1 - yl) * 4 + x

    def along(e):
        return yl * 4 + (x + e) % 4

    def first_y(j):
        return remote(part_y.at[j, pl.ds((1 - yl) * 4, 4)], got_y.at[j], ya_s.at[j], ya_r.at[j], s, across)

    def second_x(j, e):
        return remote(mid_y.at[j, e], end_y.at[j, e], yb_s.at[j, e], yb_r.at[j, e], s, along(e))

    def first_x(j, e):
        return remote(
            part_x.at[j, pl.ds((x + e) % 4 * 2, 2)], got_x.at[j, e], xa_s.at[j, e], xa_r.at[j, e], s, along(e)
        )

    def second_y(j):
        return remote(mid_x.at[j, 1 - yl], end_x.at[j], xb_s.at[j], xb_r.at[j], s, across)

    def project(j, turns):
        lhs = jnp.concatenate(
            [jnp.concatenate([g_ref[q, zz] for zz in range(Z)], axis=1) for q in (2 * j, 2 * j + 1)], axis=0
        )
        for e in turns:
            there = (x + e) % 4
            rhs = jnp.concatenate([w_ref[there], w_ref[4 + there]], axis=1)
            value = jnp.dot(lhs, rhs, preferred_element_type=F32).astype(BF16)
            for n in range(2):
                part_y[j, n * 4 + there] = value[0:B, n * B : (n + 1) * B]
                part_x[j, there * 2 + n] = value[B : 2 * B, n * B : (n + 1) * B]
            if e:
                first_x(j, e).start()
            else:
                first_y(j).start()

    def middle(j):
        first_y(j).wait_recv()
        for e in (2, 1, 3, 0):
            there = (x + e) % 4
            total = part_y[j, yl * 4 + there].astype(F32) + got_y[j, there].astype(F32)
            mid_y[j, e] = total.astype(BF16)
            if e:
                second_x(j, e).start()
        for e in (1, 2, 3):
            first_x(j, e).wait_recv()
        for n in range(2):
            total = part_x[j, x * 2 + n].astype(F32)
            for e in (1, 2, 3):
                total = total + got_x[j, e, n].astype(F32)
            mid_x[j, n] = total.astype(BF16)
        second_y(j).start()

    def to_plane(j, q):
        owner = j + 4 * q
        return owner, remote(sum_ref.at[j, q], plane_ref.at[z], z_s.at[j, q], z_r.at[z], owner * 2 + half, k)

    def collect(j):
        for q in range(2):
            if q == 0:
                total = mid_y[j, 0].astype(F32)
                for e in (1, 2, 3):
                    second_x(j, e).wait_recv()
                    total = total + end_y[j, e].astype(F32)
            else:
                second_y(j).wait_recv()
                total = mid_x[j, yl].astype(F32) + end_x[j].astype(F32)
            sum_ref[j, q] = total.astype(BF16)
            owner, copy = to_plane(j, q)

            @pl.when(z != owner)
            def _():
                copy.start()

            @pl.when(z == owner)
            def _():
                plane_ref[owner] = sum_ref[j, q]

    own(0)
    own(1)
    own(2)
    own(3)
    fetch(1).start()
    fetch(0).wait_recv()
    share(0).start()
    forward(0, 1)
    forward(1, 1)
    forward(2, 1)
    forward(3, 1)
    forward(0, 2)
    forward(1, 2)
    forward(2, 2)
    forward(3, 2)
    fetch(1).wait_recv()
    share(1).start()
    forward(0, 3)
    forward(1, 3)
    forward(2, 3)
    forward(3, 3)
    forward(0, 4)
    share(0).wait_recv()
    share(1).wait_recv()
    project(0, (2, 1, 3, 0))
    forward(1, 4)
    project(1, (2, 1, 3, 0))
    forward(2, 4)
    project(2, (2, 1, 3, 0))
    forward(3, 4)
    project(3, (2, 1, 3, 0))
    middle(0)
    middle(1)
    middle(2)
    middle(3)
    collect(0)
    collect(1)
    collect(2)
    collect(3)

    for zz in range(Z):

        @pl.when(z != zz)
        def _():
            remote(sum_ref.at[0, 0], plane_ref.at[zz], z_s.at[0, 0], z_r.at[zz], zz * 2 + half, k).wait_recv()

        @pl.when(k != zz)
        def _():
            remote(plane_ref.at[zz], last_ref.at[k], f_s.at[zz], f_r.at[k], s, zz).start()

        @pl.when(k == zz)
        def _():
            last_ref[zz] = plane_ref[zz]

    for kk in range(CHAN):

        @pl.when(k != kk)
        def _():
            remote(plane_ref.at[0], last_ref.at[kk], f_s.at[0], f_r.at[kk], s, kk).wait_recv()

        cols = slice(kk * B, (kk + 1) * B)
        out_ref[:, cols] = (last_ref[kk].astype(F32) + look_ref[:, cols].astype(F32)).astype(BF16)

    for copy in mate:
        copy.wait_send()
    for n in range(2):
        fetch(n).wait_send()
        share(n).wait_send()
    for c in range(4):
        for n in range(1, 5):
            if up_has(c, n):
                up(c, n).wait_send()
            if down_has(c, n):
                down(c, n).wait_send()
    for j in range(4):
        first_y(j).wait_send()
        second_y(j).wait_send()
        for e in (1, 2, 3):
            first_x(j, e).wait_send()
            second_x(j, e).wait_send()
    for j in range(4):
        for q in range(2):
            owner, copy = to_plane(j, q)

            @pl.when(z != owner)
            def _():
                copy.wait_send()

    for zz in range(Z):

        @pl.when(k != zz)
        def _():
            remote(plane_ref.at[zz], last_ref.at[k], f_s.at[zz], f_r.at[k], s, zz).wait_send()


def local(features, lengths, ids, taps, filters, skip, out_weight, embedding):
    vmem = pl.BlockSpec(memory_space=pltpu.VMEM)
    hbm = pl.BlockSpec(memory_space=pl.ANY)
    dma = pltpu.SemaphoreType.DMA
    tile = (B, B)
    return pl.pallas_call(
        kernel,
        out_shape=jax.ShapeDtypeStruct((B, CHAN * B), BF16),
        in_specs=[pl.BlockSpec(memory_space=pltpu.SMEM), hbm, vmem, hbm, vmem, hbm, vmem, hbm],
        out_specs=vmem,
        scratch_shapes=[
            pltpu.VMEM((3, B, CHAN * B), BF16),
            pltpu.VMEM((OWN, LAGS * B), F32),
            pltpu.VMEM((16, CHAN * B), BF16),
            pltpu.VMEM((16, CHAN * B), BF16),
            pltpu.VMEM((SEQ,) + tile, BF16),
            pltpu.VMEM((SEQ,) + tile, BF16),
            pltpu.VMEM((OWN, (LAGS + 1) * B, B), BF16),
            pltpu.VMEM(((LAGS + SEQ + 1) * PITCH, B), F32),
            pltpu.VMEM(((SEQ + 1) * PITCH, B), F32),
            pltpu.VMEM((2, 8, OWN, B), BF16),
            pltpu.VMEM((8, 2, OWN, B), BF16),
            pltpu.VMEM((CHAN, CHAN * B, B), BF16),
            pltpu.VMEM(embedding.shape, BF16),
            pltpu.VMEM((8, Z) + tile, BF16),
            pltpu.VMEM((4, CHAN) + tile, BF16),
            pltpu.VMEM((4, CHAN) + tile, BF16),
            pltpu.VMEM((4, 4) + tile, BF16),
            pltpu.VMEM((4, 4, 2) + tile, BF16),
            pltpu.VMEM((4, 4) + tile, BF16),
            pltpu.VMEM((4, 2) + tile, BF16),
            pltpu.VMEM((4, 4) + tile, BF16),
            pltpu.VMEM((4,) + tile, BF16),
            pltpu.VMEM((4, 2) + tile, BF16),
            pltpu.VMEM((Z,) + tile, BF16),
            pltpu.VMEM((CHAN,) + tile, BF16),
            pltpu.VMEM((B, CHAN * B), BF16),
            dma((4,)), dma, dma, dma,
            dma, dma, dma((2,)), dma((2,)), dma((2,)), dma((2,)),
            dma((Z, 2)), dma((Z, 2)), dma((Z, 2)), dma((Z, 2)),
            dma((Z,)), dma((Z,)),
            dma((4, 5)), dma((4, 5)), dma((4, 5)), dma((4, 5)),
            dma((4,)), dma((4,)), dma((4, 4)), dma((4, 4)), dma((4, 4)), dma((4, 4)), dma((4,)), dma((4,)),
            dma((4, 2)), dma((Z,)),
            dma((Z,)), dma((CHAN,)),
        ],
        compiler_params=pltpu.CompilerParams(
            collective_id=0, has_side_effects=True, vmem_limit_bytes=56 * 2**20
        ),
        name="hyena_block",
    )(
        lengths,
        features.transpose(1, 0, 2),
        taps,
        filters,
        skip.reshape(1, -1),
        out_weight,
        ids.reshape(1, -1),
        embedding,
    )


def solution(mesh):
    placed = (
        P(("dp", "seq"), None, "chan"),
        P("dp"),
        P(("dp", "seq")),
        P(None, None, "chan"),
        P(("chan", "seq"), None),
        P(("chan", "seq")),
        P("chan", "seq"),
        P(None, "chan"),
    )
    return jax.shard_map(
        local, mesh=mesh, in_specs=placed, out_specs=P(("dp", "seq"), "chan"), check_vma=False
    )
```
